512 devices in a mesh: seg: 128 (over y, z, core), head: 4 (over x).
Axes of the slice: x: 4, y: 8, z: 8, core: 2. Of those that a mesh axis runs over, the one named last changes fastest.
Arguments:
- inputs: bfloat16 [256, 512, 1024], P('seg', None, 'head'), may hold values from -0.25 to 0.25
- cotangent: bfloat16 [256, 512, 1024], P('seg', None, 'head'), may hold values from -0.25 to 0.25
- state_in: bfloat16 [256, 512, 128], P('seg'), may hold values from -1.75 to 1.75
- state_out: bfloat16 [256, 512, 128], P('seg'), may hold values from -1.75 to 1.75
- log_decay: float32 [256, 16, 512], P('seg', 'head'), may hold values from -1 to 0
- parents: int32 [256], replicated, may hold values from -1 to 7, as said below
- slot_segment: int32 [256], replicated, may hold values from 0 to 255, as said below
Outputs:
- grad_inputs: bfloat16 [256, 512, 1024], P('seg', None, 'head')
- grad_state_in: float32 [256, 512, 128], P('seg', 'head')
- grad_state_out: float32 [256, 512, 128], P('seg', 'head')
The draws below stay inside these ranges and needn't reach their ends.
Inputs may be any that keep to these rules, and one draw needn't show every extreme that they name: parents[s] is -1 for s < 2; each of the next 6 segments has a parent below 2; every other segment has a parent from 2 to 7; every segment below 8 has a child. `slot_segment`: each segment is held in exactly one slot.
All inputs are finite; a program needn't handle non-finite values.
Results may differ from the reference program's by a relative error of at most 0.0085.
Values sent between devices are 32-bit elements; how exact they have to be, the bound alone decides.
A program may use at most 64 MiB of HBM per device.

```python
import math
import jax
import jax.numpy as jnp
from jax import lax

HEAD_DIM = 64
STATE = 128
HEADS = 16
PIECE_POSITIONS = 512
SEG_DEV = 2
SEGS = 256
ROOTS = 2
MIDS = 6


def draw_log_decay(key, part):
    key = jax.random.fold_in(key, 5)
    sampler_seeds = jax.random.split(key, 6)
    grid_extents = (SEGS, HEADS, PIECE_POSITIONS)
    slow = jnp.exp(jax.random.uniform(sampler_seeds[0], (SEGS, HEADS, 1), jnp.float32, math.log(0.3), math.log(1.2))) / (3.0 * PIECE_POSITIONS)
    fast = jnp.exp(jax.random.uniform(sampler_seeds[1], (SEGS, HEADS, 1), jnp.float32, math.log(1.0 / 50.0), math.log(1.0 / 30.0)))
    share = 0.5
    quick = jax.random.uniform(sampler_seeds[2], (SEGS, HEADS, 1), jnp.float32) < share
    forgetting_factor = jnp.where(quick, fast, slow)
    approximate_guess = jax.random.uniform(sampler_seeds[3], grid_extents, jnp.float32, 0.5, 2.0)
    span_count = (jax.random.uniform(sampler_seeds[4], grid_extents, jnp.float32) < 0.5 / PIECE_POSITIONS).astype(jnp.float32)
    hierarchy_levels = jax.random.uniform(sampler_seeds[5], grid_extents, jnp.float32, 0.22, 0.69)
    return -(forgetting_factor * approximate_guess + span_count * hierarchy_levels)


def draw_parents(key, part):
    key = jax.random.fold_in(key, 11)
    sampler_seeds = jax.random.split(key, 3)
    index = jnp.arange(SEGS, dtype=jnp.int32)
    mid_random = jax.random.randint(sampler_seeds[0], (SEGS,), 0, ROOTS, jnp.int32)
    mid_offset = index - ROOTS
    mid_parent = jnp.where(mid_offset < 3, 0, jnp.where(mid_offset < ROOTS + 2, mid_offset - 2, mid_random))
    leaf_first = jax.random.randint(sampler_seeds[1], (SEGS,), 0, MIDS, jnp.int32)
    leaf_second = jax.random.randint(sampler_seeds[2], (SEGS,), 0, MIDS, jnp.int32)
    leaf_offset = index - ROOTS - MIDS
    leaf_parent = ROOTS + jnp.where(leaf_offset < MIDS, jnp.maximum(leaf_offset, 0) % MIDS, jnp.minimum(leaf_first, leaf_second))
    result = jnp.where(index < ROOTS, -1, jnp.where(index < ROOTS + MIDS, mid_parent, leaf_parent))
    return result.astype(jnp.int32)


def place_segment(order, segment_id, slot):
    everyone = jnp.arange(SEGS, dtype=jnp.int32)
    where_now = jnp.sum(jnp.where(order == segment_id, everyone, 0)).astype(jnp.int32)
    occupant = order[slot]
    order = order.at[where_now].set(occupant)
    return order.at[slot].set(segment_id)


def draw_slot_segment(key, part):
    key = jax.random.fold_in(key, 17)
    sampler_seeds = jax.random.split(key, 3)
    device_count = SEGS // SEG_DEV
    order = jax.random.permutation(sampler_seeds[0], jnp.arange(SEGS, dtype=jnp.int32)).astype(jnp.int32)
    anchor = jax.random.randint(sampler_seeds[1], (), 0, device_count, jnp.int32)
    offsets = jax.random.randint(sampler_seeds[2], (4,), 0, SEG_DEV, jnp.int32)
    devices = jnp.stack([anchor, (anchor + device_count - 1) % device_count, (anchor + device_count // 2) % device_count, (anchor + 1) % device_count]).astype(jnp.int32)
    slots = (devices * SEG_DEV + offsets).astype(jnp.int32)
    order = place_segment(order, 0, slots[0])
    order = place_segment(order, ROOTS, slots[1])
    order = place_segment(order, ROOTS + 1, slots[2])
    order = place_segment(order, ROOTS + 2, slots[3])
    return order.astype(jnp.int32)


def steps_of(stream_key, extent, shards, smallest, high):
    gain, own = 1.0, jax.random.fold_in(stream_key, 6)
    for dim, shards_of in shards:
        heights = jnp.exp(jax.random.uniform(jax.random.fold_in(own, dim), (shards_of,), jnp.float32, smallest / len(shards), high / len(shards)))
        gain = gain * jnp.repeat(heights, extent[dim] // shards_of).reshape([-1 if axis == dim else 1 for axis in range(len(extent))])
    return gain


def centred(rng, shape, width, most, cuts=(), held_as=jnp.bfloat16):
    drawn = jax.random.normal(rng, shape, jnp.float32) * width
    if len(cuts) > 0:
        drawn = steps_of(rng, shape, cuts, -0.22, 0.18) * drawn
    return jnp.clip(drawn, min=-most, max=most).astype(held_as)


def setup_inputs(seed: int = 0) -> dict:
    keys = jax.random.split(jax.random.key(seed), 8)
    return {
        "inputs": centred(keys[0], (SEGS, PIECE_POSITIONS, HEADS * HEAD_DIM), (PIECE_POSITIONS ** -0.5), 0.25, ((0, 128), (2, 4))),
        "cotangent": centred(keys[1], (SEGS, PIECE_POSITIONS, HEADS * HEAD_DIM), (PIECE_POSITIONS ** -0.5), 0.25, ((0, 128), (2, 4))),
        "state_in": centred(keys[2], (SEGS, PIECE_POSITIONS, STATE), (STATE ** -0.25), 1.75, ((0, 128),)),
        "state_out": centred(keys[3], (SEGS, PIECE_POSITIONS, STATE), (STATE ** -0.25), 1.75, ((0, 128),)),
        "log_decay": draw_log_decay(jax.random.fold_in(keys[7], 71), 0),
        "parents": draw_parents(jax.random.fold_in(keys[7], 71), 0),
        "slot_segment": draw_slot_segment(jax.random.fold_in(keys[7], 71), 0),
    }


def causal_decay(cumulative):
    length = cumulative.shape[1]
    later = jnp.arange(length)[:, None] >= jnp.arange(length)[None, :]
    spread = cumulative[:, :, None] - cumulative[:, None, :]
    return jnp.where(later[None], jnp.exp(jnp.where(later[None], spread, 0.0)), 0.0)


def segment_local(sliced):
    inputs_s, cotan_s, sin_s, sout_s, decay_s = sliced
    length = inputs_s.shape[0]
    head_count = decay_s.shape[0]
    head_width = inputs_s.shape[1] // head_count
    cumulative = jnp.cumsum(decay_s, axis=1)
    to_end = jnp.exp(cumulative[:, -1:] - cumulative)
    from_start = jnp.exp(cumulative)
    input_heads = inputs_s.reshape(length, head_count, head_width).astype(jnp.float32)
    cotan_heads = cotan_s.reshape(length, head_count, head_width).astype(jnp.float32)
    scaled_in = (input_heads * to_end.T[:, :, None]).astype(jnp.bfloat16)
    scaled_cot = (cotan_heads * from_start.T[:, :, None]).astype(jnp.bfloat16)
    local_end = jnp.einsum("lhp,ln->hpn", scaled_in.astype(jnp.float32), sin_s.astype(jnp.float32))
    local_adj = jnp.einsum("lhp,ln->hpn", scaled_cot.astype(jnp.float32), sout_s.astype(jnp.float32))
    return local_end, local_adj, jnp.exp(cumulative[:, -1])


def segment_grads(sliced):
    inputs_s, cotan_s, sin_s, sout_s, decay_s, start_state, adjoint_end = sliced
    length = inputs_s.shape[0]
    head_count = decay_s.shape[0]
    head_width = inputs_s.shape[1] // head_count
    cumulative = jnp.cumsum(decay_s, axis=1)
    to_end = jnp.exp(cumulative[:, -1:] - cumulative)
    from_start = jnp.exp(cumulative)
    input_heads = inputs_s.reshape(length, head_count, head_width).astype(jnp.float32)
    cotan_heads = cotan_s.reshape(length, head_count, head_width).astype(jnp.float32)
    sin_full = sin_s.astype(jnp.float32)
    sout_full = sout_s.astype(jnp.float32)
    scores = jnp.dot(sout_s, sin_s.T, preferred_element_type=jnp.float32)
    decay_mask = causal_decay(cumulative)
    weights = (decay_mask * scores[None]).astype(jnp.bfloat16)
    quad_in = jnp.einsum("htu,thp->uhp", weights.astype(jnp.float32), cotan_heads)
    state_in_term = to_end.T[:, :, None] * jnp.einsum("un,hpn->uhp", sin_full, adjoint_end, precision=lax.Precision.HIGHEST)
    grad_in = (quad_in + state_in_term).astype(jnp.bfloat16).reshape(length, head_count * head_width)
    products = jnp.einsum("thp,uhp->htu", cotan_heads, input_heads)
    coupled = (decay_mask * products).astype(jnp.bfloat16).astype(jnp.float32)
    write_quad = jnp.einsum("htu,tn->un", coupled, sout_full)
    read_quad = jnp.einsum("htu,un->tn", coupled, sin_full)
    write_state = jnp.sum(to_end.T[:, :, None] * jnp.einsum("uhp,hpn->uhn", input_heads, adjoint_end, precision=lax.Precision.HIGHEST), axis=1)
    read_state = jnp.sum(from_start.T[:, :, None] * jnp.einsum("thp,hpn->thn", cotan_heads, start_state, precision=lax.Precision.HIGHEST), axis=1)
    return grad_in, write_quad + write_state, read_quad + read_state


def reference(inputs, cotangent, state_in, state_out, log_decay, parents, slot_segment):
    slot_count = inputs.shape[0]
    local_end, local_adj, end_decay = lax.map(segment_local, (inputs, cotangent, state_in, state_out, log_decay))
    position = jnp.zeros((slot_count,), jnp.int32).at[slot_segment].set(jnp.arange(slot_count, dtype=jnp.int32))
    end_seg = local_end[position]
    adj_seg = local_adj[position]
    decay_seg = end_decay[position][:, :, None, None]
    has_parent = (parents >= 0)[:, None, None, None]
    safe_parent = jnp.maximum(parents, 0).astype(jnp.int32)
    start_seg = jnp.zeros_like(end_seg)
    for sweep in range(2):
        end_states = decay_seg * start_seg + end_seg
        start_seg = jnp.where(has_parent, end_states[safe_parent], 0.0)
    target = jnp.where(parents >= 0, parents, slot_count).astype(jnp.int32)
    adjoint_seg = jnp.zeros_like(adj_seg)
    for sweep in range(2):
        begin_adj = adj_seg + decay_seg * adjoint_seg
        adjoint_seg = jax.ops.segment_sum(begin_adj, target, num_segments=slot_count + 1)[:slot_count]
    start_slot = start_seg[slot_segment]
    adjoint_slot = adjoint_seg[slot_segment]
    grad_inputs, grad_state_in, grad_state_out = lax.map(segment_grads, (inputs, cotangent, state_in, state_out, log_decay, start_slot, adjoint_slot))
    return grad_inputs, grad_state_in, grad_state_out
```

```python
import jax
import jax.numpy as jnp
from jax import lax
from jax.experimental import pallas as pl
from jax.experimental.pallas import tpu as pltpu
from jax.sharding import PartitionSpec as P

MESH = pl.DeviceIdType.MESH
F32 = jnp.float32
BF16 = jnp.bfloat16

ROOTS = 2
TABLE = 8
RING = 8
CORES = 2
HEAD_DEVS = 4
SEG_DEV = 2
LENGTH = 512
HEADS_DEV = 4
HEAD_DIM = 64
WIDTH = HEADS_DEV * HEAD_DIM
STATE = 128
SLICE = STATE // RING
BLOCK = 128


def dot(a, b):
    return jnp.dot(a, b, preferred_element_type=F32)


def dot_nt(a, b):
    return lax.dot_general(a, b, (((1,), (1,)), ((), ())), preferred_element_type=F32)


def dot_tn(a, b):
    return lax.dot_general(a, b, (((0,), (0,)), ((), ())), preferred_element_type=F32)


def seg_index(y, z, c):
    return (y * RING + z) * CORES + c


def split(value):
    upper = value.astype(BF16)
    return upper, (value - upper.astype(F32)).astype(BF16)


def kernel(
    inputs, cotan, sin, sout, ldec, parents, slots,
    grad_in, grad_sin, grad_sout,
    cum_row, cum_col, weight_end, scaled_in, scaled_cot, quad_in, part,
    send1f, recv1f, send1j, recv1j, send2f, recv2f, send2j, recv2j,
    send3, recv3, table, send4, recv4, recvx,
    ss1, rs1, ss2, rs2, ss3, rs3, ss4, rs4, ssx, rsx,
):
    s = lax.axis_index("seg")
    x = lax.axis_index("head")
    c = lax.rem(s, CORES)
    z = lax.rem(s // CORES, RING)
    y = s // (CORES * RING)

    mine = (y, z)
    other = (z, y)

    def first_peer(half, i):
        if half == 0:
            return seg_index(lax.rem(y + i, RING), z, c)
        return seg_index(y, lax.rem(z + i, RING), c)

    def second_peer(half, i, k):
        ck = lax.rem(c + k, CORES)
        if half == 0:
            return seg_index(y, lax.rem(z + i, RING), ck)
        return seg_index(lax.rem(y + i, RING), z, ck)

    def source_seg(half, i):
        if half == 0:
            return seg_index(lax.rem(y + RING - i, RING), z, c)
        return seg_index(y, lax.rem(z + RING - i, RING), c)

    barrier = pltpu.get_barrier_semaphore()
    peers = []
    for half in range(2):
        for i in range(1, RING):
            for k in range(CORES):
                peers.append((second_peer(half, i, k), x))
    peers.append((seg_index(y, z, lax.rem(c + 1, CORES)), x))
    for i in range(1, HEAD_DEVS):
        peers.append((s, lax.rem(x + i, HEAD_DEVS)))
    for peer in peers:
        pl.semaphore_signal(barrier, inc=1, device_id=peer, device_id_type=MESH)

    copies = []

    def send(src, dst, ssem, rsem, peer):
        copy = pltpu.make_async_remote_copy(
            src_ref=src, dst_ref=dst, send_sem=ssem, recv_sem=rsem,
            device_id=peer, device_id_type=MESH,
        )
        copy.start()
        copies.append(copy)
        return copy

    rows = SEG_DEV * HEADS_DEV
    blocks = LENGTH // BLOCK
    decay = jnp.concatenate([ldec[q] for q in range(SEG_DEV)], axis=0)
    stacked = jnp.concatenate([decay[:, b * BLOCK : (b + 1) * BLOCK] for b in range(blocks)], axis=0)
    top, rest = stacked.astype(BF16), None
    rest = stacked - top.astype(F32)
    middle, low = split(rest)
    earlier = lax.broadcasted_iota(jnp.int32, (BLOCK, BLOCK), 0)
    later = lax.broadcasted_iota(jnp.int32, (BLOCK, BLOCK), 1)
    causal = earlier <= later
    ones = jnp.where(causal, 1.0, 0.0).astype(BF16)
    sums = dot(low, ones) + dot(middle, ones) + dot(top, ones)
    base = jnp.zeros((rows, 1), F32)
    pieces = []
    for b in range(blocks):
        piece = sums[b * rows : (b + 1) * rows] + base
        pieces.append(piece)
        base = piece[:, BLOCK - 1 : BLOCK]
    cumulative = jnp.concatenate(pieces, axis=1)
    cum_row[...] = cumulative
    columns = jnp.concatenate(
        [jnp.exp(base - cumulative), jnp.exp(cumulative), cumulative, jnp.zeros_like(cumulative)], axis=0
    )
    columns = jnp.transpose(columns)
    cum_col[...] = columns
    upper, lower = split(columns)
    key_row = lax.broadcasted_iota(jnp.int32, (4 * rows, 2 * WIDTH), 0)
    key_lane = lax.broadcasted_iota(jnp.int32, (4 * rows, 2 * WIDTH), 1)
    for q in range(SEG_DEV):
        wanted = (key_lane // WIDTH) * rows + q * HEADS_DEV + lax.rem(key_lane, WIDTH) // HEAD_DIM
        pick = jnp.where(key_row == wanted, 1.0, 0.0).astype(BF16)
        spread = dot(upper, pick) + dot(lower, pick)
        to_end, from_start = spread[:, :WIDTH], spread[:, WIDTH:]
        weight_end[q] = to_end
        s_in = (inputs[q].astype(F32) * to_end).astype(BF16)
        s_cot = (cotan[q].astype(F32) * from_start).astype(BF16)
        scaled_in[q] = s_in
        scaled_cot[q] = s_cot
        local_end = dot_tn(sin[q], s_in)
        local_adj = dot_tn(sout[q], s_cot)
        end_decay = from_start[LENGTH - 1 : LENGTH]
        for half in range(2):
            lanes = slice(half * BLOCK, (half + 1) * BLOCK)
            place = pl.ds(q * SLICE, SLICE)
            send1f[half, :, place, :] = local_end[:, lanes].reshape(RING, SLICE, BLOCK)
            send1j[half, :, place, :] = local_adj[:, lanes].reshape(RING, SLICE, BLOCK)
            tile = jnp.broadcast_to(end_decay[:, lanes].reshape(1, 1, BLOCK), (RING, 8, BLOCK))
            send1f[half, :, pl.ds(SEG_DEV * SLICE + 8 * q, 8), :] = tile

    pl.semaphore_wait(barrier, len(peers))

    got1 = []
    for chunk, (out, into) in enumerate(((send1f, recv1f), (send1j, recv1j))):
        for i in range(1, RING):
            for half in range(2):
                to = lax.rem(mine[half] + i, RING)
                got1.append((chunk, send(
                    out.at[half, to], into.at[half, i],
                    ss1.at[chunk, half, i], rs1.at[chunk, half, i], (first_peer(half, i), x),
                )))
    for half in range(2):
        recv1f[half, 0] = send1f[half, mine[half]]
        recv1j[half, 0] = send1j[half, mine[half]]

    lane = lax.broadcasted_iota(jnp.int32, (BLOCK, BLOCK), 1)
    first_head = lane < HEAD_DIM
    for q in range(SEG_DEV):
        for b in range(blocks):
            u0 = b * BLOCK
            length = LENGTH - u0
            here = pl.ds(u0, BLOCK)
            onward = pl.ds(u0, length)
            sin_b = sin[q, here]
            sout_b = sout[q, onward]
            scores = dot_nt(sin_b, sout_b)
            coupled = None
            for pair in range(HEADS_DEV // 2):
                lanes = pl.ds(pair * BLOCK, BLOCK)
                in_pair = inputs[q, here, lanes]
                cot_pair = cotan[q, onward, lanes]
                results = []
                for k in range(2):
                    r = q * HEADS_DEV + pair * 2 + k
                    col = 2 * rows + r
                    spread = cum_row[r : r + 1, onward] - cum_col[here, col : col + 1]
                    mask = jnp.where(causal, jnp.exp(jnp.where(causal, spread[:, :BLOCK], 0.0)), 0.0)
                    if length > BLOCK:
                        mask = jnp.concatenate([mask, jnp.exp(spread[:, BLOCK:])], axis=1)
                    weights = (mask * scores).astype(BF16)
                    results.append(dot(weights, cot_pair))
                    own = first_head if k == 0 else jnp.logical_not(first_head)
                    in_head = jnp.where(own, in_pair.astype(F32), 0.0).astype(BF16)
                    term = mask * dot_nt(in_head, cot_pair)
                    coupled = term if coupled is None else coupled + term
                quad_in[q, here, lanes] = jnp.where(first_head, results[0], results[1])
            coupled = coupled.astype(BF16)
            part[0, q, here] = dot(coupled, sout_b)
            read = dot_tn(coupled, sin_b)
            if b == 0:
                part[1, q] = read
            else:
                part[1, q, onward] = part[1, q, onward] + read

    rank = lax.broadcasted_iota(jnp.int32, (TABLE, SLICE, BLOCK), 0)
    rank_row = lax.broadcasted_iota(jnp.int32, (TABLE, BLOCK), 0)
    got2 = []
    for chunk in range(2):
        for owner, copy in got1:
            if owner == chunk:
                copy.wait_recv()
        for half in range(2):
            total = jnp.zeros((TABLE, SLICE, BLOCK), F32)
            decays = jnp.zeros((TABLE, BLOCK), F32)
            for i in range(RING):
                for q in range(SEG_DEV):
                    segment = slots[source_seg(half, i) * SEG_DEV + q]
                    place = pl.ds(q * SLICE, SLICE)
                    if chunk == 0:
                        total = total + jnp.where(rank == segment, recv1f[half, i, place][None], 0.0)
                        row = recv1f[half, i, pl.ds(SEG_DEV * SLICE + 8 * q, 8)]
                        decays = decays + jnp.where(rank_row == segment, row, 0.0)
                    else:
                        parent = parents[segment]
                        total = total + jnp.where(rank == parent, recv1j[half, i, place][None], 0.0)
            out = send2f if chunk == 0 else send2j
            for k in range(TABLE):
                out[half, :, k, :] = total[k]
            if chunk == 0:
                out[half, :, pl.ds(TABLE, TABLE), :] = jnp.broadcast_to(
                    decays[None], (SLICE, TABLE, BLOCK)
                )
        out, into = ((send2f, recv2f), (send2j, recv2j))[chunk]
        for i in range(RING):
            for k in range(CORES):
                for half in range(2):
                    to = lax.rem(other[half] + i, RING) * CORES + lax.rem(c + k, CORES)
                    slot = i * CORES + k
                    if slot == 0:
                        into[half, 0] = out[half, to]
                        continue
                    got2.append((chunk, send(
                        out.at[half, to], into.at[half, slot],
                        ss2.at[chunk, half, slot], rs2.at[chunk, half, slot],
                        (second_peer(half, i, k), x),
                    )))

    got3 = []
    decays = [None, None]
    for chunk in range(2):
        for owner, copy in got2:
            if owner == chunk:
                copy.wait_recv()
        for half in range(2):
            into = recv2f if chunk == 0 else recv2j
            total = into[half, 0]
            for slot in range(1, SLICE):
                total = total + into[half, slot]
            if chunk == 0:
                decays[half] = total[TABLE:]
                carried = jnp.zeros((TABLE, BLOCK), F32)
                for m in range(ROOTS, TABLE):
                    start = jnp.where(parents[m] == 0, total[0:1], total[1:2])
                    carried = carried + jnp.where(rank_row == m, start, 0.0)
                send3[chunk, half] = total[:TABLE] + decays[half] * carried
            else:
                carried = jnp.zeros((TABLE, BLOCK), F32)
                product = decays[half] * total
                for m in range(ROOTS, TABLE):
                    carried = carried + jnp.where(rank_row == parents[m], product[m : m + 1], 0.0)
                send3[chunk, half] = total + jnp.where(rank_row < ROOTS, carried, 0.0)
        for i in range(RING):
            for k in range(CORES):
                for half in range(2):
                    row = other[half] * CORES + c
                    slot = i * CORES + k
                    if slot == 0:
                        recv3[chunk, half, row] = send3[chunk, half]
                        continue
                    got3.append((chunk, send(
                        send3.at[chunk, half], recv3.at[chunk, half, row],
                        ss3.at[chunk, half, slot], rs3.at[chunk, half, slot],
                        (second_peer(half, i, k), x),
                    )))

    got4 = []
    for chunk in range(2):
        for owner, copy in got3:
            if owner == chunk:
                copy.wait_recv()
        for half in range(2):
            for k in range(TABLE):
                table[chunk, half, k] = recv3[chunk, half, :, k, :]
            for i in range(RING):
                to = lax.rem(mine[half] + i, RING)
                for q in range(SEG_DEV):
                    segment = slots[first_peer(half, i) * SEG_DEV + q]
                    if chunk == 0:
                        index = parents[segment]
                        exists = index >= 0
                        index = jnp.maximum(index, 0)
                    else:
                        exists = segment < TABLE
                        index = jnp.minimum(segment, TABLE - 1)
                    picked = table[chunk, half, index]
                    send4[chunk, half, i, q] = jnp.where(exists, picked, 0.0)
        for i in range(RING):
            for half in range(2):
                row = mine[half]
                if i == 0:
                    recv4[chunk, half, row] = send4[chunk, half, 0]
                    continue
                got4.append((chunk, send(
                    send4.at[chunk, half, i], recv4.at[chunk, half, row],
                    ss4.at[chunk, half, i], rs4.at[chunk, half, i], (first_peer(half, i), x),
                )))

    gotx = []
    for chunk in range(2):
        for owner, copy in got4:
            if owner == chunk:
                copy.wait_recv()
        kind = 1 - chunk
        states = []
        for q in range(SEG_DEV):
            halves = [recv4[chunk, half, :, q].reshape(STATE, BLOCK) for half in range(2)]
            state = jnp.concatenate(halves, axis=1).astype(BF16)
            states.append(state)
            data = scaled_cot[q] if chunk == 0 else scaled_in[q]
            part[kind, q] = part[kind, q] + dot_nt(data, state)
        for i in range(1, HEAD_DEVS):
            to = lax.rem(x + i, HEAD_DEVS)
            piece = pl.ds(pl.multiple_of(to * BLOCK, BLOCK), BLOCK)
            gotx.append((chunk, send(
                part.at[kind, :, piece], recvx.at[kind, i], ssx.at[kind, i], rsx.at[kind, i], (s, to)
            )))
        if chunk == 1:
            for q in range(SEG_DEV):
                term = weight_end[q] * dot(sin[q], states[q])
                grad_in[q] = (quad_in[q] + term).astype(BF16)
    own = pl.ds(pl.multiple_of(x * BLOCK, BLOCK), BLOCK)
    for chunk in range(2):
        for owner, copy in gotx:
            if owner == chunk:
                copy.wait_recv()
        kind = 1 - chunk
        total = part[kind, :, own]
        for i in range(1, HEAD_DEVS):
            total = total + recvx[kind, i]
        result = grad_sin if kind == 0 else grad_sout
        result[...] = total
    for copy in copies:
        copy.wait_send()


def shards(inputs, cotangent, state_in, state_out, log_decay, parents, slot_segment):
    vmem = pl.BlockSpec(memory_space=pltpu.VMEM)
    smem = pl.BlockSpec(memory_space=pltpu.SMEM)
    both = SEG_DEV * HEADS_DEV
    slots2 = RING * CORES
    dma = pltpu.SemaphoreType.DMA
    return pl.pallas_call(
        kernel,
        out_shape=(
            jax.ShapeDtypeStruct(inputs.shape, BF16),
            jax.ShapeDtypeStruct((SEG_DEV, BLOCK, STATE), F32),
            jax.ShapeDtypeStruct((SEG_DEV, BLOCK, STATE), F32),
        ),
        in_specs=[vmem] * 5 + [smem] * 2,
        out_specs=(vmem, vmem, vmem),
        scratch_shapes=[
            pltpu.VMEM((both, LENGTH), F32),
            pltpu.VMEM((LENGTH, 4 * both), F32),
            pltpu.VMEM((SEG_DEV, LENGTH, WIDTH), F32),
            pltpu.VMEM((SEG_DEV, LENGTH, WIDTH), BF16),
            pltpu.VMEM((SEG_DEV, LENGTH, WIDTH), BF16),
            pltpu.VMEM((SEG_DEV, LENGTH, WIDTH), F32),
            pltpu.VMEM((2, SEG_DEV, LENGTH, STATE), F32),
            pltpu.VMEM((2, RING, SEG_DEV * (SLICE + 8), BLOCK), F32),
            pltpu.VMEM((2, RING, SEG_DEV * (SLICE + 8), BLOCK), F32),
            pltpu.VMEM((2, RING, SEG_DEV * SLICE, BLOCK), F32),
            pltpu.VMEM((2, RING, SEG_DEV * SLICE, BLOCK), F32),
            pltpu.VMEM((2, SLICE, 2 * TABLE, BLOCK), F32),
            pltpu.VMEM((2, slots2, 2 * TABLE, BLOCK), F32),
            pltpu.VMEM((2, SLICE, TABLE, BLOCK), F32),
            pltpu.VMEM((2, slots2, TABLE, BLOCK), F32),
            pltpu.VMEM((2, 2, TABLE, BLOCK), F32),
            pltpu.VMEM((2, 2, SLICE, TABLE, BLOCK), F32),
            pltpu.VMEM((2, 2, TABLE, SLICE, BLOCK), F32),
            pltpu.VMEM((2, 2, RING, SEG_DEV, SLICE, BLOCK), F32),
            pltpu.VMEM((2, 2, RING, SEG_DEV, SLICE, BLOCK), F32),
            pltpu.VMEM((2, HEAD_DEVS, SEG_DEV, BLOCK, STATE), F32),
            dma((2, 2, RING)), dma((2, 2, RING)),
            dma((2, 2, slots2)), dma((2, 2, slots2)),
            dma((2, 2, slots2)), dma((2, 2, slots2)),
            dma((2, 2, RING)), dma((2, 2, RING)),
            dma((2, HEAD_DEVS)), dma((2, HEAD_DEVS)),
        ],
        compiler_params=pltpu.CompilerParams(
            collective_id=0, has_side_effects=True, vmem_limit_bytes=40 * 2**20
        ),
    )(inputs, cotangent, state_in, state_out, log_decay, parents, slot_segment)


def solution(mesh):
    placed = (
        P("seg", None, "head"),
        P("seg", None, "head"),
        P("seg", None, None),
        P("seg", None, None),
        P("seg", "head", None),
        P(),
        P(),
    )
    return jax.shard_map(
        shards,
        mesh=mesh,
        in_specs=placed,
        out_specs=(P("seg", None, "head"), P("seg", "head", None), P("seg", "head", None)),
        check_vma=False,
    )
```

```python
import jax
import jax.numpy as jnp
from jax import lax
from jax.experimental import pallas as pl
from jax.experimental.pallas import tpu as pltpu
from jax.sharding import PartitionSpec as P

MESH = pl.DeviceIdType.MESH
F32 = jnp.float32
BF16 = jnp.bfloat16

ROOTS = 2
TABLE = 8
RING = 8
CORES = 2
HEAD_DEVS = 4
SEG_DEV = 2
LENGTH = 512
HEADS_DEV = 4
HEAD_DIM = 64
WIDTH = HEADS_DEV * HEAD_DIM
STATE = 128
SLICE = STATE // RING
BLOCK = 128
ROW1 = SEG_DEV * SLICE


def dot(a, b):
    return jnp.dot(a, b, preferred_element_type=F32)


def dot_nt(a, b):
    return lax.dot_general(a, b, (((1,), (1,)), ((), ())), preferred_element_type=F32)


def dot_tn(a, b):
    return lax.dot_general(a, b, (((0,), (0,)), ((), ())), preferred_element_type=F32)


def seg_index(y, z, c):
    return (y * RING + z) * CORES + c


def split(value):
    upper = value.astype(BF16)
    return upper, (value - upper.astype(F32)).astype(BF16)


def kernel(
    inputs_hbm, cotan_hbm, sin_hbm, sout_hbm, ldec_hbm, parents_hbm, slots_hbm,
    grad_in, grad_sin, grad_sout,
    inputs, cotan, sin, sout, ldec, parents, slots, lsem,
    cum_row, cum_col, weight_end, scaled_in, scaled_cot, quad_in, part,
    send1f, recv1f, send1j, recv1j, send2f, recv2f, send2j, recv2j,
    send3, recv3, table, send4, recv4, recvx,
    out_in, out_sin, out_sout, sent, arrived, osem,
):
    s = lax.axis_index("seg")
    x = lax.axis_index("head")
    c = lax.rem(s, CORES)
    z = lax.rem(s // CORES, RING)
    y = s // (CORES * RING)

    mine = (y, z)
    other = (z, y)

    def first_peer(half, i):
        if half == 0:
            return seg_index(lax.rem(y + i, RING), z, c)
        return seg_index(y, lax.rem(z + i, RING), c)

    def second_peer(half, i, k):
        ck = lax.rem(c + k, CORES)
        if half == 0:
            return seg_index(y, lax.rem(z + i, RING), ck)
        return seg_index(lax.rem(y + i, RING), z, ck)

    def source_seg(half, i):
        if half == 0:
            return seg_index(lax.rem(y + RING - i, RING), z, c)
        return seg_index(y, lax.rem(z + RING - i, RING), c)

    loads = []
    operands = (
        (ldec_hbm, ldec), (inputs_hbm, inputs), (cotan_hbm, cotan), (sin_hbm, sin),
        (sout_hbm, sout), (slots_hbm, slots), (parents_hbm, parents),
    )
    for n, (far, near) in enumerate(operands):
        load = pltpu.make_async_copy(far, near, lsem.at[n])
        load.start()
        loads.append(load)

    barrier = pltpu.get_barrier_semaphore()
    peers = []
    for half in range(2):
        for i in range(1, RING):
            for k in range(CORES):
                peers.append((second_peer(half, i, k), x))
    peers.append((seg_index(y, z, lax.rem(c + 1, CORES)), x))
    for i in range(1, HEAD_DEVS):
        peers.append((s, lax.rem(x + i, HEAD_DEVS)))
    for peer in peers:
        pl.semaphore_signal(barrier, inc=1, device_id=peer, device_id_type=MESH)

    pending = []

    def send(src, dst, stage, peer):
        pltpu.make_async_remote_copy(
            src_ref=src, dst_ref=dst, send_sem=sent.at[stage], recv_sem=arrived.at[stage],
            device_id=peer, device_id_type=MESH,
        ).start()

    def arrive(stage, whole):
        copy = pltpu.make_async_remote_copy(
            src_ref=whole, dst_ref=whole, send_sem=sent.at[stage], recv_sem=arrived.at[stage],
            device_id=(seg_index(y, z, lax.rem(c + 1, CORES)), x), device_id_type=MESH,
        )
        copy.wait_recv()
        pending.append(copy)

    loads[0].wait()
    rows = SEG_DEV * HEADS_DEV
    blocks = LENGTH // BLOCK
    decay = jnp.concatenate([ldec[q] for q in range(SEG_DEV)], axis=0)
    stacked = jnp.concatenate([decay[:, b * BLOCK : (b + 1) * BLOCK] for b in range(blocks)], axis=0)
    top, rest = stacked.astype(BF16), None
    rest = stacked - top.astype(F32)
    middle, low = split(rest)
    earlier = lax.broadcasted_iota(jnp.int32, (BLOCK, BLOCK), 0)
    later = lax.broadcasted_iota(jnp.int32, (BLOCK, BLOCK), 1)
    causal = earlier <= later
    ones = jnp.where(causal, 1.0, 0.0).astype(BF16)
    sums = dot(low, ones) + dot(middle, ones) + dot(top, ones)
    base = jnp.zeros((rows, 1), F32)
    pieces = []
    for b in range(blocks):
        piece = sums[b * rows : (b + 1) * rows] + base
        pieces.append(piece)
        base = piece[:, BLOCK - 1 : BLOCK]
    cumulative = jnp.concatenate(pieces, axis=1)
    cum_row[...] = cumulative
    columns = jnp.concatenate(
        [jnp.exp(base - cumulative), jnp.exp(cumulative), cumulative, jnp.zeros_like(cumulative)], axis=0
    )
    columns = jnp.transpose(columns)
    cum_col[...] = columns
    upper, lower = split(columns)
    for load in loads[1:]:
        load.wait()
    key_row = lax.broadcasted_iota(jnp.int32, (4 * rows, 2 * WIDTH), 0)
    key_lane = lax.broadcasted_iota(jnp.int32, (4 * rows, 2 * WIDTH), 1)
    lane64 = lax.rem(lax.broadcasted_iota(jnp.int32, (1, WIDTH), 1), HEAD_DIM)
    packed = None
    for q in range(SEG_DEV):
        wanted = (key_lane // WIDTH) * rows + q * HEADS_DEV + lax.rem(key_lane, WIDTH) // HEAD_DIM
        pick = jnp.where(key_row == wanted, 1.0, 0.0).astype(BF16)
        spread = dot(upper, pick) + dot(lower, pick)
        to_end, from_start = spread[:, :WIDTH], spread[:, WIDTH:]
        weight_end[q] = to_end
        s_in = (inputs[q].astype(F32) * to_end).astype(BF16)
        s_cot = (cotan[q].astype(F32) * from_start).astype(BF16)
        scaled_in[q] = s_in
        scaled_cot[q] = s_cot
        local_end = dot_tn(sin[q], s_in)
        local_adj = dot_tn(sout[q], s_cot)
        segment = slots[s * SEG_DEV + q]
        end_decay = jnp.where(lane64 == segment, from_start[LENGTH - 1 : LENGTH], 0.0)
        packed = end_decay if q == 0 else packed + end_decay
        for half in range(2):
            lanes = slice(half * BLOCK, (half + 1) * BLOCK)
            place = pl.ds(q * SLICE, SLICE)
            send1f[half, :, place, :] = local_end[:, lanes].reshape(RING, SLICE, BLOCK)
            send1j[half, :, place, :] = local_adj[:, lanes].reshape(RING, SLICE, BLOCK)
    for half in range(2):
        row = packed[:, half * BLOCK : (half + 1) * BLOCK].reshape(1, 1, BLOCK)
        send1f[half, :, pl.ds(ROW1, 1), :] = jnp.broadcast_to(row, (RING, 1, BLOCK))

    pl.semaphore_wait(barrier, len(peers))

    rows1 = (pl.ds(0, ROW1 + 1), pl.ds(0, ROW1))
    out1, in1 = (send1f, send1j), (recv1f, recv1j)
    for chunk in range(2):
        for i in range(1, RING):
            for half in range(2):
                to = lax.rem(mine[half] + i, RING)
                send(
                    out1[chunk].at[half, to, rows1[chunk]], in1[chunk].at[half, i, rows1[chunk]],
                    chunk, (first_peer(half, i), x),
                )
    for half in range(2):
        recv1f[half, 0, rows1[0]] = send1f[half, mine[half], rows1[0]]
        recv1j[half, 0] = send1j[half, mine[half]]

    lane = lax.broadcasted_iota(jnp.int32, (BLOCK, BLOCK), 1)
    first_head = lane < HEAD_DIM
    for q in range(SEG_DEV):
        for b in range(blocks):
            u0 = b * BLOCK
            length = LENGTH - u0
            here = pl.ds(u0, BLOCK)
            onward = pl.ds(u0, length)
            sin_b = sin[q, here]
            sout_b = sout[q, onward]
            scores = dot_nt(sin_b, sout_b)
            coupled = None
            for pair in range(HEADS_DEV // 2):
                lanes = pl.ds(pair * BLOCK, BLOCK)
                in_pair = inputs[q, here, lanes]
                cot_pair = cotan[q, onward, lanes]
                results = []
                for k in range(2):
                    r = q * HEADS_DEV + pair * 2 + k
                    col = 2 * rows + r
                    spread = cum_row[r : r + 1, onward] - cum_col[here, col : col + 1]
                    mask = jnp.where(causal, jnp.exp(jnp.where(causal, spread[:, :BLOCK], 0.0)), 0.0)
                    if length > BLOCK:
                        mask = jnp.concatenate([mask, jnp.exp(spread[:, BLOCK:])], axis=1)
                    weights = (mask * scores).astype(BF16)
                    results.append(dot(weights, cot_pair))
                    own = first_head if k == 0 else jnp.logical_not(first_head)
                    in_head = jnp.where(own, in_pair.astype(F32), 0.0).astype(BF16)
                    term = mask * dot_nt(in_head, cot_pair)
                    coupled = term if coupled is None else coupled + term
                quad_in[q, here, lanes] = jnp.where(first_head, results[0], results[1])
            coupled = coupled.astype(BF16)
            part[0, q, here] = dot(coupled, sout_b)
            read = dot_tn(coupled, sin_b)
            if b == 0:
                part[1, q] = read
            else:
                part[1, q, onward] = part[1, q, onward] + read

    rank = lax.broadcasted_iota(jnp.int32, (TABLE, SLICE, BLOCK), 0)
    rank_row = lax.broadcasted_iota(jnp.int32, (TABLE, BLOCK), 0)
    rank_lane = lax.rem(lane[:TABLE], HEAD_DIM)
    left = lane[:TABLE] < HEAD_DIM
    rows2 = (pl.ds(0, TABLE + 1), pl.ds(0, TABLE))
    out2, in2 = (send2f, send2j), (recv2f, recv2j)
    decays = [None, None]

    def second(chunk):
        arrive(chunk, in1[chunk].at[:, pl.ds(1, RING - 1), rows1[chunk]])
        out, into = out2[chunk], in2[chunk]
        for half in range(2):
            total = jnp.zeros((TABLE, SLICE, BLOCK), F32)
            for i in range(RING):
                for q in range(SEG_DEV):
                    index = slots[source_seg(half, i) * SEG_DEV + q]
                    if chunk == 1:
                        index = parents[index]
                    block = in1[chunk][half, i, pl.ds(q * SLICE, SLICE)]
                    total = total + jnp.where(rank == index, block[None], 0.0)
            for k in range(TABLE):
                out[half, :, k, :] = total[k]
            if chunk == 0:
                row = recv1f[half, 0, pl.ds(ROW1, 1)]
                for i in range(1, RING):
                    row = row + recv1f[half, i, pl.ds(ROW1, 1)]
                out[half, :, pl.ds(TABLE, 1), :] = jnp.broadcast_to(
                    row.reshape(1, 1, BLOCK), (SLICE, 1, BLOCK)
                )
        for i in range(RING):
            for k in range(CORES):
                for half in range(2):
                    to = lax.rem(other[half] + i, RING) * CORES + lax.rem(c + k, CORES)
                    slot = i * CORES + k
                    if slot == 0:
                        into[half, 0, rows2[chunk]] = out[half, to, rows2[chunk]]
                        continue
                    send(
                        out.at[half, to, rows2[chunk]], into.at[half, slot, rows2[chunk]],
                        2 + chunk, (second_peer(half, i, k), x),
                    )

    def third(chunk):
        into = in2[chunk]
        arrive(2 + chunk, into.at[:, pl.ds(1, SLICE - 1), rows2[chunk]])
        for half in range(2):
            total = into[half, 0, pl.ds(0, TABLE)]
            for slot in range(1, SLICE):
                total = total + into[half, slot, pl.ds(0, TABLE)]
            if chunk == 0:
                row = into[half, 0, pl.ds(TABLE, 1)]
                for slot in range(1, SLICE):
                    row = row + into[half, slot, pl.ds(TABLE, 1)]
                spread = jnp.where(rank_lane == rank_row, row, 0.0)
                first = jnp.sum(jnp.where(left, spread, 0.0), axis=1, keepdims=True)
                second_head = jnp.sum(jnp.where(left, 0.0, spread), axis=1, keepdims=True)
                decays[half] = jnp.where(left, first, second_head)
                carried = jnp.zeros((TABLE, BLOCK), F32)
                for m in range(ROOTS, TABLE):
                    start = jnp.where(parents[m] == 0, total[0:1], total[1:2])
                    carried = carried + jnp.where(rank_row == m, start, 0.0)
                send3[chunk, half] = total + decays[half] * carried
            else:
                carried = jnp.zeros((TABLE, BLOCK), F32)
                product = decays[half] * total
                for m in range(ROOTS, TABLE):
                    carried = carried + jnp.where(rank_row == parents[m], product[m : m + 1], 0.0)
                send3[chunk, half] = total + jnp.where(rank_row < ROOTS, carried, 0.0)
        for i in range(RING):
            for k in range(CORES):
                for half in range(2):
                    row = other[half] * CORES + c
                    if i + k == 0:
                        recv3[chunk, half, row] = send3[chunk, half]
                        continue
                    send(
                        send3.at[chunk, half], recv3.at[chunk, half, row],
                        4 + chunk, (second_peer(half, i, k), x),
                    )

    def fourth(chunk):
        arrive(4 + chunk, recv3.at[chunk, :, pl.ds(0, SLICE - 1)])
        for half in range(2):
            for k in range(TABLE):
                table[chunk, half, k] = recv3[chunk, half, :, k, :]
            for i in range(RING):
                for q in range(SEG_DEV):
                    segment = slots[first_peer(half, i) * SEG_DEV + q]
                    if chunk == 0:
                        index = parents[segment]
                        exists = index >= 0
                        index = jnp.maximum(index, 0)
                    else:
                        exists = segment < TABLE
                        index = jnp.minimum(segment, TABLE - 1)
                    picked = table[chunk, half, index]
                    send4[chunk, half, i, q] = jnp.where(exists, picked, 0.0)
        for i in range(RING):
            for half in range(2):
                row = mine[half]
                if i == 0:
                    recv4[chunk, half, row] = send4[chunk, half, 0]
                    continue
                send(
                    send4.at[chunk, half, i], recv4.at[chunk, half, row],
                    6 + chunk, (first_peer(half, i), x),
                )

    def states_of(chunk):
        arrive(6 + chunk, recv4.at[chunk, :, pl.ds(0, RING - 1)])
        kind = 1 - chunk
        states = []
        for q in range(SEG_DEV):
            halves = [recv4[chunk, half, :, q].reshape(STATE, BLOCK) for half in range(2)]
            state = jnp.concatenate(halves, axis=1).astype(BF16)
            states.append(state)
            data = scaled_cot[q] if chunk == 0 else scaled_in[q]
            part[kind, q] = part[kind, q] + dot_nt(data, state)
        for i in range(1, HEAD_DEVS):
            to = lax.rem(x + i, HEAD_DEVS)
            piece = pl.ds(pl.multiple_of(to * BLOCK, BLOCK), BLOCK)
            send(part.at[kind, :, piece], recvx.at[kind, i], 8 + chunk, (s, to))
        return states

    own = pl.ds(pl.multiple_of(x * BLOCK, BLOCK), BLOCK)

    def heads_of(chunk):
        kind = 1 - chunk
        arrive(8 + chunk, recvx.at[kind, pl.ds(1, HEAD_DEVS - 1)])
        total = part[kind, :, own]
        for i in range(1, HEAD_DEVS):
            total = total + recvx[kind, i]
        near, far = ((out_sin, grad_sin), (out_sout, grad_sout))[kind]
        near[...] = total
        return pltpu.make_async_copy(near, far, osem.at[kind])

    second(0)
    third(0)
    second(1)
    fourth(0)
    third(1)
    states_of(0)
    fourth(1)
    adjoints = states_of(1)
    for q in range(SEG_DEV):
        term = weight_end[q] * dot(sin[q], adjoints[q])
        out_in[q] = (quad_in[q] + term).astype(BF16)
    stores = [pltpu.make_async_copy(out_in, grad_in, osem.at[2])]
    stores[0].start()
    for chunk in range(2):
        stores.append(heads_of(chunk))
        stores[-1].start()
    for store in stores:
        store.wait()
    for copy in pending:
        copy.wait_send()


def hand_over(a_in, b_in, c_in, a_out, b_out, c_out, a, b, c, isem, osem):
    pairs = ((a_in, a), (b_in, b), (c_in, c))
    loads = [pltpu.make_async_copy(far, near, isem.at[n]) for n, (far, near) in enumerate(pairs)]
    pairs = ((a, a_out), (b, b_out), (c, c_out))
    stores = [pltpu.make_async_copy(near, far, osem.at[n]) for n, (near, far) in enumerate(pairs)]
    for load in loads:
        load.start()
    for load, store in zip(loads, stores):
        load.wait()
        store.start()
    for store in stores:
        store.wait()


def shards(inputs, cotangent, state_in, state_out, log_decay, parents, slot_segment):
    hbm = pl.BlockSpec(memory_space=pltpu.HBM)
    both = SEG_DEV * HEADS_DEV
    slots2 = RING * CORES
    dma = pltpu.SemaphoreType.DMA
    grad_state = (SEG_DEV, BLOCK, STATE)
    shapes = (
        jax.ShapeDtypeStruct(inputs.shape, BF16),
        jax.ShapeDtypeStruct(grad_state, F32),
        jax.ShapeDtypeStruct(grad_state, F32),
    )
    results = pl.pallas_call(
        kernel,
        out_shape=shapes,
        in_specs=[hbm] * 7,
        out_specs=(hbm,) * 3,
        scratch_shapes=[
            pltpu.VMEM(inputs.shape, BF16),
            pltpu.VMEM(inputs.shape, BF16),
            pltpu.VMEM(state_in.shape, BF16),
            pltpu.VMEM(state_in.shape, BF16),
            pltpu.VMEM(log_decay.shape, F32),
            pltpu.SMEM(parents.shape, jnp.int32),
            pltpu.SMEM(parents.shape, jnp.int32),
            dma((7,)),
            pltpu.VMEM((both, LENGTH), F32),
            pltpu.VMEM((LENGTH, 4 * both), F32),
            pltpu.VMEM((SEG_DEV, LENGTH, WIDTH), F32),
            pltpu.VMEM((SEG_DEV, LENGTH, WIDTH), BF16),
            pltpu.VMEM((SEG_DEV, LENGTH, WIDTH), BF16),
            pltpu.VMEM((SEG_DEV, LENGTH, WIDTH), F32),
            pltpu.VMEM((2, SEG_DEV, LENGTH, STATE), F32),
            pltpu.VMEM((2, RING, ROW1 + 8, BLOCK), F32),
            pltpu.VMEM((2, RING, ROW1 + 8, BLOCK), F32),
            pltpu.VMEM((2, RING, ROW1, BLOCK), F32),
            pltpu.VMEM((2, RING, ROW1, BLOCK), F32),
            pltpu.VMEM((2, SLICE, 2 * TABLE, BLOCK), F32),
            pltpu.VMEM((2, slots2, 2 * TABLE, BLOCK), F32),
            pltpu.VMEM((2, SLICE, TABLE, BLOCK), F32),
            pltpu.VMEM((2, slots2, TABLE, BLOCK), F32),
            pltpu.VMEM((2, 2, TABLE, BLOCK), F32),
            pltpu.VMEM((2, 2, SLICE, TABLE, BLOCK), F32),
            pltpu.VMEM((2, 2, TABLE, SLICE, BLOCK), F32),
            pltpu.VMEM((2, 2, RING, SEG_DEV, SLICE, BLOCK), F32),
            pltpu.VMEM((2, 2, RING, SEG_DEV, SLICE, BLOCK), F32),
            pltpu.VMEM((2, HEAD_DEVS, SEG_DEV, BLOCK, STATE), F32),
            pltpu.VMEM(inputs.shape, BF16),
            pltpu.VMEM(grad_state, F32),
            pltpu.VMEM(grad_state, F32),
            dma((10,)), dma((10,)), dma((3,)),
        ],
        compiler_params=pltpu.CompilerParams(
            collective_id=0, has_side_effects=True, vmem_limit_bytes=60 * 2**20
        ),
    )(inputs, cotangent, state_in, state_out, log_decay, parents, slot_segment)
    return pl.pallas_call(
        hand_over,
        out_shape=shapes,
        in_specs=[hbm] * 3,
        out_specs=(hbm,) * 3,
        scratch_shapes=[pltpu.VMEM(r.shape, r.dtype) for r in results] + [dma((3,)), dma((3,))],
        compiler_params=pltpu.CompilerParams(vmem_limit_bytes=60 * 2**20),
    )(*results)


def solution(mesh):
    placed = (
        P("seg", None, "head"),
        P("seg", None, "head"),
        P("seg", None, None),
        P("seg", None, None),
        P("seg", "head", None),
        P(),
        P(),
    )
    return jax.shard_map(
        shards,
        mesh=mesh,
        in_specs=placed,
        out_specs=(P("seg", None, "head"), P("seg", "head", None), P("seg", "head", None)),
        check_vma=False,
    )
```

```python
import jax
import jax.numpy as jnp
from jax import lax
from jax.experimental import pallas as pl
from jax.experimental.pallas import tpu as pltpu
from jax.sharding import PartitionSpec as P

MESH = pl.DeviceIdType.MESH
F32 = jnp.float32
BF16 = jnp.bfloat16

ROOTS = 2
TABLE = 8
RING = 8
ORDER = (4, 3, 5, 2, 6, 1, 7, 0)
CORES = 2
HEAD_DEVS = 4
SEG_DEV = 2
LENGTH = 512
HEADS_DEV = 4
HEAD_DIM = 64
WIDTH = HEADS_DEV * HEAD_DIM
STATE = 128
SLICE = STATE // RING
BLOCK = 128
ADJ_AFTER = 1
ROW1 = SEG_DEV * SLICE


def dot(a, b):
    return jnp.dot(a, b, preferred_element_type=F32)


def dot_nt(a, b):
    return lax.dot_general(a, b, (((1,), (1,)), ((), ())), preferred_element_type=F32)


def dot_tn(a, b):
    return lax.dot_general(a, b, (((0,), (0,)), ((), ())), preferred_element_type=F32)


def seg_index(y, z, c):
    return (y * RING + z) * CORES + c


def split(value):
    upper = value.astype(BF16)
    return upper, (value - upper.astype(F32)).astype(BF16)


def kernel(
    inputs_hbm, cotan_hbm, sin_hbm, sout_hbm, ldec_hbm, parents_hbm, slots_hbm,
    grad_in, grad_sin, grad_sout,
    inputs, cotan, sin, sout, ldec, parents, slots, lsem,
    cum_row, cum_col, weight_end, scaled_in, scaled_cot, quad_in, part,
    send1f, recv1f, send1j, recv1j, send2f, recv2f, send2j, recv2j,
    send3, recv3, table, send4, recv4, recvx,
    out_in, out_sin, out_sout, sent, arrived, osem,
):
    s = lax.axis_index("seg")
    x = lax.axis_index("head")
    c = lax.rem(s, CORES)
    z = lax.rem(s // CORES, RING)
    y = s // (CORES * RING)

    mine = (y, z)
    other = (z, y)

    def first_peer(half, i):
        if half == 0:
            return seg_index(lax.rem(y + i, RING), z, c)
        return seg_index(y, lax.rem(z + i, RING), c)

    def second_peer(half, i, k):
        ck = lax.rem(c + k, CORES)
        if half == 0:
            return seg_index(y, lax.rem(z + i, RING), ck)
        return seg_index(lax.rem(y + i, RING), z, ck)

    def source_seg(half, i):
        if half == 0:
            return seg_index(lax.rem(y + RING - i, RING), z, c)
        return seg_index(y, lax.rem(z + RING - i, RING), c)

    loads = []
    operands = (
        (ldec_hbm, ldec), (inputs_hbm, inputs), (cotan_hbm, cotan), (sin_hbm, sin),
        (sout_hbm, sout), (slots_hbm, slots), (parents_hbm, parents),
    )
    for n, (far, near) in enumerate(operands):
        load = pltpu.make_async_copy(far, near, lsem.at[n])
        load.start()
        loads.append(load)

    barrier = pltpu.get_barrier_semaphore()
    peers = []
    for half in range(2):
        for i in range(1, RING):
            for k in range(CORES):
                peers.append((second_peer(half, i, k), x))
    peers.append((seg_index(y, z, lax.rem(c + 1, CORES)), x))
    for i in range(1, HEAD_DEVS):
        peers.append((s, lax.rem(x + i, HEAD_DEVS)))
    for peer in peers:
        pl.semaphore_signal(barrier, inc=1, device_id=peer, device_id_type=MESH)

    pending = []

    def send(src, dst, stage, peer):
        pltpu.make_async_remote_copy(
            src_ref=src, dst_ref=dst, send_sem=sent.at[stage], recv_sem=arrived.at[stage],
            device_id=peer, device_id_type=MESH,
        ).start()

    def arrive(stage, whole):
        copy = pltpu.make_async_remote_copy(
            src_ref=whole, dst_ref=whole, send_sem=sent.at[stage], recv_sem=arrived.at[stage],
            device_id=(seg_index(y, z, lax.rem(c + 1, CORES)), x), device_id_type=MESH,
        )
        copy.wait_recv()
        pending.append(copy)

    loads[0].wait()
    rows = SEG_DEV * HEADS_DEV
    blocks = LENGTH // BLOCK
    decay = jnp.concatenate([ldec[q] for q in range(SEG_DEV)], axis=0)
    stacked = jnp.concatenate([decay[:, b * BLOCK : (b + 1) * BLOCK] for b in range(blocks)], axis=0)
    top, rest = stacked.astype(BF16), None
    rest = stacked - top.astype(F32)
    middle, low = split(rest)
    earlier = lax.broadcasted_iota(jnp.int32, (BLOCK, BLOCK), 0)
    later = lax.broadcasted_iota(jnp.int32, (BLOCK, BLOCK), 1)
    causal = earlier <= later
    ones = jnp.where(causal, 1.0, 0.0).astype(BF16)
    sums = dot(low, ones) + dot(middle, ones) + dot(top, ones)
    base = jnp.zeros((rows, 1), F32)
    pieces = []
    for b in range(blocks):
        piece = sums[b * rows : (b + 1) * rows] + base
        pieces.append(piece)
        base = piece[:, BLOCK - 1 : BLOCK]
    cumulative = jnp.concatenate(pieces, axis=1)
    cum_row[...] = cumulative
    columns = jnp.concatenate(
        [jnp.exp(base - cumulative), jnp.exp(cumulative), cumulative, jnp.zeros_like(cumulative)], axis=0
    )
    columns = jnp.transpose(columns)
    cum_col[...] = columns
    upper, lower = split(columns)
    for load in loads[1:]:
        load.wait()
    key_row = lax.broadcasted_iota(jnp.int32, (4 * rows, 2 * WIDTH), 0)
    key_lane = lax.broadcasted_iota(jnp.int32, (4 * rows, 2 * WIDTH), 1)
    lane64 = lax.rem(lax.broadcasted_iota(jnp.int32, (1, WIDTH), 1), HEAD_DIM)
    packed = None
    for q in range(SEG_DEV):
        wanted = (key_lane // WIDTH) * rows + q * HEADS_DEV + lax.rem(key_lane, WIDTH) // HEAD_DIM
        pick = jnp.where(key_row == wanted, 1.0, 0.0).astype(BF16)
        spread = dot(upper, pick) + dot(lower, pick)
        to_end, from_start = spread[:, :WIDTH], spread[:, WIDTH:]
        weight_end[q] = to_end
        s_in = (inputs[q].astype(F32) * to_end).astype(BF16)
        s_cot = (cotan[q].astype(F32) * from_start).astype(BF16)
        scaled_in[q] = s_in
        scaled_cot[q] = s_cot
        local_end = dot_tn(sin[q], s_in)
        local_adj = dot_tn(sout[q], s_cot)
        segment = slots[s * SEG_DEV + q]
        end_decay = jnp.where(lane64 == segment, from_start[LENGTH - 1 : LENGTH], 0.0)
        packed = end_decay if q == 0 else packed + end_decay
        for half in range(2):
            lanes = slice(half * BLOCK, (half + 1) * BLOCK)
            place = pl.ds(q * SLICE, SLICE)
            send1f[half, :, place, :] = local_end[:, lanes].reshape(RING, SLICE, BLOCK)
            send1j[half, :, place, :] = local_adj[:, lanes].reshape(RING, SLICE, BLOCK)
    for half in range(2):
        row = packed[:, half * BLOCK : (half + 1) * BLOCK].reshape(1, 1, BLOCK)
        send1f[half, :, pl.ds(ROW1, 1), :] = jnp.broadcast_to(row, (RING, 1, BLOCK))

    pl.semaphore_wait(barrier, len(peers))

    rows1 = (pl.ds(0, ROW1 + 1), pl.ds(0, ROW1))
    out1, in1 = (send1f, send1j), (recv1f, recv1j)

    def first(chunk):
        for i in ORDER[:-1]:
            for half in range(2):
                to = lax.rem(mine[half] + i, RING)
                send(
                    out1[chunk].at[half, to, rows1[chunk]], in1[chunk].at[half, i, rows1[chunk]],
                    chunk, (first_peer(half, i), x),
                )
        for half in range(2):
            in1[chunk][half, 0, rows1[chunk]] = out1[chunk][half, mine[half], rows1[chunk]]

    first(0)

    lane = lax.broadcasted_iota(jnp.int32, (BLOCK, BLOCK), 1)
    first_head = lane < HEAD_DIM
    for q in range(SEG_DEV):
        for b in range(blocks):
            u0 = b * BLOCK
            length = LENGTH - u0
            here = pl.ds(u0, BLOCK)
            onward = pl.ds(u0, length)
            sin_b = sin[q, here]
            sout_b = sout[q, onward]
            scores = dot_nt(sin_b, sout_b)
            coupled = None
            for pair in range(HEADS_DEV // 2):
                lanes = pl.ds(pair * BLOCK, BLOCK)
                in_pair = inputs[q, here, lanes]
                cot_pair = cotan[q, onward, lanes]
                results = []
                for k in range(2):
                    r = q * HEADS_DEV + pair * 2 + k
                    col = 2 * rows + r
                    spread = cum_row[r : r + 1, onward] - cum_col[here, col : col + 1]
                    mask = jnp.where(causal, jnp.exp(jnp.where(causal, spread[:, :BLOCK], 0.0)), 0.0)
                    if length > BLOCK:
                        mask = jnp.concatenate([mask, jnp.exp(spread[:, BLOCK:])], axis=1)
                    weights = (mask * scores).astype(BF16)
                    results.append(dot(weights, cot_pair))
                    own = first_head if k == 0 else jnp.logical_not(first_head)
                    in_head = jnp.where(own, in_pair.astype(F32), 0.0).astype(BF16)
                    term = mask * dot_nt(in_head, cot_pair)
                    coupled = term if coupled is None else coupled + term
                quad_in[q, here, lanes] = jnp.where(first_head, results[0], results[1])
            if q == 0 and b == ADJ_AFTER:
                first(1)
            coupled = coupled.astype(BF16)
            part[0, q, here] = dot(coupled, sout_b)
            read = dot_tn(coupled, sin_b)
            if b == 0:
                part[1, q] = read
            else:
                part[1, q, onward] = part[1, q, onward] + read

    rank = lax.broadcasted_iota(jnp.int32, (TABLE, SLICE, BLOCK), 0)
    rank_row = lax.broadcasted_iota(jnp.int32, (TABLE, BLOCK), 0)
    rank_lane = lax.rem(lane[:TABLE], HEAD_DIM)
    left = lane[:TABLE] < HEAD_DIM
    rows2 = (pl.ds(0, TABLE + 1), pl.ds(0, TABLE))
    out2, in2 = (send2f, send2j), (recv2f, recv2j)
    decays = [None, None]

    def second(chunk):
        arrive(chunk, in1[chunk].at[:, pl.ds(1, RING - 1), rows1[chunk]])
        out, into = out2[chunk], in2[chunk]
        for half in range(2):
            total = jnp.zeros((TABLE, SLICE, BLOCK), F32)
            for i in range(RING):
                for q in range(SEG_DEV):
                    index = slots[source_seg(half, i) * SEG_DEV + q]
                    if chunk == 1:
                        index = parents[index]
                    block = in1[chunk][half, i, pl.ds(q * SLICE, SLICE)]
                    total = total + jnp.where(rank == index, block[None], 0.0)
            for k in range(TABLE):
                out[half, :, k, :] = total[k]
            if chunk == 0:
                row = recv1f[half, 0, pl.ds(ROW1, 1)]
                for i in range(1, RING):
                    row = row + recv1f[half, i, pl.ds(ROW1, 1)]
                out[half, :, pl.ds(TABLE, 1), :] = jnp.broadcast_to(
                    row.reshape(1, 1, BLOCK), (SLICE, 1, BLOCK)
                )
            for i in ORDER:
                for k in range(CORES):
                    to = lax.rem(other[half] + i, RING) * CORES + lax.rem(c + k, CORES)
                    slot = i * CORES + k
                    if slot == 0:
                        into[half, 0, rows2[chunk]] = out[half, to, rows2[chunk]]
                        continue
                    send(
                        out.at[half, to, rows2[chunk]], into.at[half, slot, rows2[chunk]],
                        2 + chunk, (second_peer(half, i, k), x),
                    )

    def third(chunk):
        into = in2[chunk]
        arrive(2 + chunk, into.at[:, pl.ds(1, SLICE - 1), rows2[chunk]])
        for half in range(2):
            total = into[half, 0, pl.ds(0, TABLE)]
            for slot in range(1, SLICE):
                total = total + into[half, slot, pl.ds(0, TABLE)]
            if chunk == 0:
                row = into[half, 0, pl.ds(TABLE, 1)]
                for slot in range(1, SLICE):
                    row = row + into[half, slot, pl.ds(TABLE, 1)]
                spread = jnp.where(rank_lane == rank_row, row, 0.0)
                first = jnp.sum(jnp.where(left, spread, 0.0), axis=1, keepdims=True)
                second_head = jnp.sum(jnp.where(left, 0.0, spread), axis=1, keepdims=True)
                decays[half] = jnp.where(left, first, second_head)
                carried = jnp.zeros((TABLE, BLOCK), F32)
                for m in range(ROOTS, TABLE):
                    start = jnp.where(parents[m] == 0, total[0:1], total[1:2])
                    carried = carried + jnp.where(rank_row == m, start, 0.0)
                send3[chunk, half] = total + decays[half] * carried
            else:
                carried = jnp.zeros((TABLE, BLOCK), F32)
                product = decays[half] * total
                for m in range(ROOTS, TABLE):
                    carried = carried + jnp.where(rank_row == parents[m], product[m : m + 1], 0.0)
                send3[chunk, half] = total + jnp.where(rank_row < ROOTS, carried, 0.0)
            row = other[half] * CORES + c
            for i in ORDER:
                for k in range(CORES):
                    if i + k == 0:
                        recv3[chunk, half, row] = send3[chunk, half]
                        continue
                    send(
                        send3.at[chunk, half], recv3.at[chunk, half, row],
                        4 + chunk, (second_peer(half, i, k), x),
                    )

    def fourth(chunk):
        arrive(4 + chunk, recv3.at[chunk, :, pl.ds(0, SLICE - 1)])
        for half in range(2):
            for k in range(TABLE):
                table[chunk, half, k] = recv3[chunk, half, :, k, :]
        for q in range(SEG_DEV):
            for i in ORDER:
                for half in range(2):
                    segment = slots[first_peer(half, i) * SEG_DEV + q]
                    if chunk == 0:
                        index = parents[segment]
                        exists = index >= 0
                        index = jnp.maximum(index, 0)
                    else:
                        exists = segment < TABLE
                        index = jnp.minimum(segment, TABLE - 1)
                    picked = jnp.where(exists, table[chunk, half, index], 0.0)
                    row = mine[half]
                    if i == 0:
                        recv4[chunk, q, half, row] = picked
                        continue
                    send4[chunk, q, half, i] = picked
                    send(
                        send4.at[chunk, q, half, i], recv4.at[chunk, q, half, row],
                        6 + 2 * chunk + q, (first_peer(half, i), x),
                    )

    def states_of(chunk):
        kind = 1 - chunk
        states = []
        for q in range(SEG_DEV):
            arrive(6 + 2 * chunk + q, recv4.at[chunk, q, :, pl.ds(0, RING - 1)])
            halves = [recv4[chunk, q, half].reshape(STATE, BLOCK) for half in range(2)]
            state = jnp.concatenate(halves, axis=1).astype(BF16)
            states.append(state)
            data = scaled_cot[q] if chunk == 0 else scaled_in[q]
            part[kind, q] = part[kind, q] + dot_nt(data, state)
            for i in (2, 1, 3):
                to = lax.rem(x + i, HEAD_DEVS)
                piece = pl.ds(pl.multiple_of(to * BLOCK, BLOCK), BLOCK)
                send(part.at[kind, q, piece], recvx.at[kind, q, i], 10 + 2 * chunk + q, (s, to))
        return states

    own = pl.ds(pl.multiple_of(x * BLOCK, BLOCK), BLOCK)

    def heads_of(chunk):
        kind = 1 - chunk
        near, far = ((out_sin, grad_sin), (out_sout, grad_sout))[kind]
        for q in range(SEG_DEV):
            arrive(10 + 2 * chunk + q, recvx.at[kind, q, pl.ds(1, HEAD_DEVS - 1)])
            total = part[kind, q, own]
            for i in range(1, HEAD_DEVS):
                total = total + recvx[kind, q, i]
            near[q] = total
            store = pltpu.make_async_copy(near.at[q], far.at[q], osem.at[2 * kind + q])
            store.start()
            stores.append(store)

    second(0)
    second(1)
    third(0)
    third(1)
    fourth(0)
    fourth(1)
    states_of(0)
    adjoints = states_of(1)
    for q in range(SEG_DEV):
        term = weight_end[q] * dot(sin[q], adjoints[q])
        out_in[q] = (quad_in[q] + term).astype(BF16)
    stores = [pltpu.make_async_copy(out_in, grad_in, osem.at[4])]
    stores[0].start()
    for chunk in range(2):
        heads_of(chunk)
    for store in stores:
        store.wait()
    for copy in pending:
        copy.wait_send()


def hand_over(a_in, b_in, c_in, a_out, b_out, c_out, a, b, c, isem, osem):
    pairs = ((a_in, a), (b_in, b), (c_in, c))
    loads = [pltpu.make_async_copy(far, near, isem.at[n]) for n, (far, near) in enumerate(pairs)]
    pairs = ((a, a_out), (b, b_out), (c, c_out))
    stores = [pltpu.make_async_copy(near, far, osem.at[n]) for n, (near, far) in enumerate(pairs)]
    for load in loads:
        load.start()
    for load, store in zip(loads, stores):
        load.wait()
        store.start()
    for store in stores:
        store.wait()


def shards(inputs, cotangent, state_in, state_out, log_decay, parents, slot_segment):
    hbm = pl.BlockSpec(memory_space=pltpu.HBM)
    both = SEG_DEV * HEADS_DEV
    slots2 = RING * CORES
    dma = pltpu.SemaphoreType.DMA
    grad_state = (SEG_DEV, BLOCK, STATE)
    shapes = (
        jax.ShapeDtypeStruct(inputs.shape, BF16),
        jax.ShapeDtypeStruct(grad_state, F32),
        jax.ShapeDtypeStruct(grad_state, F32),
    )
    results = pl.pallas_call(
        kernel,
        out_shape=shapes,
        in_specs=[hbm] * 7,
        out_specs=(hbm,) * 3,
        scratch_shapes=[
            pltpu.VMEM(inputs.shape, BF16),
            pltpu.VMEM(inputs.shape, BF16),
            pltpu.VMEM(state_in.shape, BF16),
            pltpu.VMEM(state_in.shape, BF16),
            pltpu.VMEM(log_decay.shape, F32),
            pltpu.SMEM(parents.shape, jnp.int32),
            pltpu.SMEM(parents.shape, jnp.int32),
            dma((7,)),
            pltpu.VMEM((both, LENGTH), F32),
            pltpu.VMEM((LENGTH, 4 * both), F32),
            pltpu.VMEM((SEG_DEV, LENGTH, WIDTH), F32),
            pltpu.VMEM((SEG_DEV, LENGTH, WIDTH), BF16),
            pltpu.VMEM((SEG_DEV, LENGTH, WIDTH), BF16),
            pltpu.VMEM((SEG_DEV, LENGTH, WIDTH), F32),
            pltpu.VMEM((2, SEG_DEV, LENGTH, STATE), F32),
            pltpu.VMEM((2, RING, ROW1 + 8, BLOCK), F32),
            pltpu.VMEM((2, RING, ROW1 + 8, BLOCK), F32),
            pltpu.VMEM((2, RING, ROW1, BLOCK), F32),
            pltpu.VMEM((2, RING, ROW1, BLOCK), F32),
            pltpu.VMEM((2, SLICE, 2 * TABLE, BLOCK), F32),
            pltpu.VMEM((2, slots2, 2 * TABLE, BLOCK), F32),
            pltpu.VMEM((2, SLICE, TABLE, BLOCK), F32),
            pltpu.VMEM((2, slots2, TABLE, BLOCK), F32),
            pltpu.VMEM((2, 2, TABLE, BLOCK), F32),
            pltpu.VMEM((2, 2, SLICE, TABLE, BLOCK), F32),
            pltpu.VMEM((2, 2, TABLE, SLICE, BLOCK), F32),
            pltpu.VMEM((2, SEG_DEV, 2, RING, SLICE, BLOCK), F32),
            pltpu.VMEM((2, SEG_DEV, 2, RING, SLICE, BLOCK), F32),
            pltpu.VMEM((2, SEG_DEV, HEAD_DEVS, BLOCK, STATE), F32),
            pltpu.VMEM(inputs.shape, BF16),
            pltpu.VMEM(grad_state, F32),
            pltpu.VMEM(grad_state, F32),
            dma((14,)), dma((14,)), dma((5,)),
        ],
        compiler_params=pltpu.CompilerParams(
            collective_id=0, has_side_effects=True, vmem_limit_bytes=60 * 2**20
        ),
    )(inputs, cotangent, state_in, state_out, log_decay, parents, slot_segment)
    return pl.pallas_call(
        hand_over,
        out_shape=shapes,
        in_specs=[hbm] * 3,
        out_specs=(hbm,) * 3,
        scratch_shapes=[pltpu.VMEM(r.shape, r.dtype) for r in results] + [dma((3,)), dma((3,))],
        compiler_params=pltpu.CompilerParams(vmem_limit_bytes=60 * 2**20),
    )(*results)


def solution(mesh):
    placed = (
        P("seg", None, "head"),
        P("seg", None, "head"),
        P("seg", None, None),
        P("seg", None, None),
        P("seg", "head", None),
        P(),
        P(),
    )
    return jax.shard_map(
        shards,
        mesh=mesh,
        in_specs=placed,
        out_specs=(P("seg", None, "head"), P("seg", "head", None), P("seg", "head", None)),
        check_vma=False,
    )
```

```python
import jax
import jax.numpy as jnp
from jax import lax
from jax.experimental import pallas as pl
from jax.experimental.pallas import tpu as pltpu
from jax.sharding import PartitionSpec as P

MESH = pl.DeviceIdType.MESH
F32 = jnp.float32
BF16 = jnp.bfloat16

ROOTS = 2
TABLE = 8
RING = 8
ORDER = (4, 3, 5, 2, 6, 1, 7, 0)
CORES = 2
HEAD_DEVS = 4
SEG_DEV = 2
LENGTH = 512
HEADS_DEV = 4
HEAD_DIM = 64
WIDTH = HEADS_DEV * HEAD_DIM
STATE = 128
SLICE = STATE // RING
BLOCK = 128
ADJ_AFTER = 1
ROW1 = SEG_DEV * SLICE


def dot(a, b):
    return jnp.dot(a, b, preferred_element_type=F32)


def dot_nt(a, b):
    return lax.dot_general(a, b, (((1,), (1,)), ((), ())), preferred_element_type=F32)


def dot_tn(a, b):
    return lax.dot_general(a, b, (((0,), (0,)), ((), ())), preferred_element_type=F32)


def seg_index(y, z, c):
    return (y * RING + z) * CORES + c


def split(value):
    upper = value.astype(BF16)
    return upper, (value - upper.astype(F32)).astype(BF16)


def kernel(
    inputs_hbm, cotan_hbm, sin_hbm, sout_hbm, ldec_hbm, parents_hbm, slots_hbm,
    grad_in, grad_sin, grad_sout,
    inputs, cotan, sin, sout, ldec, parents, slots, lsem,
    cum_row, cum_col, weight_end, scaled_in, scaled_cot, quad_in, part,
    send1f, recv1f, send1j, recv1j, send2f, recv2f, send2j, recv2j,
    send3, recv3, table, send4, recv4, recvx,
    out_in, out_sin, out_sout, sent, arrived, osem,
):
    s = lax.axis_index("seg")
    x = lax.axis_index("head")
    c = lax.rem(s, CORES)
    z = lax.rem(s // CORES, RING)
    y = s // (CORES * RING)

    mine = (y, z)
    other = (z, y)

    def first_peer(half, i):
        if half == 0:
            return seg_index(lax.rem(y + i, RING), z, c)
        return seg_index(y, lax.rem(z + i, RING), c)

    def second_peer(half, i, k):
        ck = lax.rem(c + k, CORES)
        if half == 0:
            return seg_index(y, lax.rem(z + i, RING), ck)
        return seg_index(lax.rem(y + i, RING), z, ck)

    def source_seg(half, i):
        if half == 0:
            return seg_index(lax.rem(y + RING - i, RING), z, c)
        return seg_index(y, lax.rem(z + RING - i, RING), c)

    loads = []
    operands = (
        (ldec_hbm, ldec), (inputs_hbm, inputs), (sin_hbm, sin), (slots_hbm, slots),
        (cotan_hbm, cotan), (sout_hbm, sout), (parents_hbm, parents),
    )
    for n, (far, near) in enumerate(operands):
        load = pltpu.make_async_copy(far, near, lsem.at[n])
        loads.append(load)
    for load in loads[:4]:
        load.start()

    barrier = pltpu.get_barrier_semaphore()
    peers = []
    for i in ORDER[:-1]:
        for half in range(2):
            for k in range(CORES):
                peers.append((second_peer(half, i, k), x))
    peers.append((seg_index(y, z, lax.rem(c + 1, CORES)), x))
    for i in range(1, HEAD_DEVS):
        peers.append((s, lax.rem(x + i, HEAD_DEVS)))
    for peer in peers:
        pl.semaphore_signal(barrier, inc=1, device_id=peer, device_id_type=MESH)
    for load in loads[4:]:
        load.start()

    pending = []

    def send(src, dst, stage, peer):
        pltpu.make_async_remote_copy(
            src_ref=src, dst_ref=dst, send_sem=sent.at[stage], recv_sem=arrived.at[stage],
            device_id=peer, device_id_type=MESH,
        ).start()

    def arrive(stage, whole):
        copy = pltpu.make_async_remote_copy(
            src_ref=whole, dst_ref=whole, send_sem=sent.at[stage], recv_sem=arrived.at[stage],
            device_id=(seg_index(y, z, lax.rem(c + 1, CORES)), x), device_id_type=MESH,
        )
        copy.wait_recv()
        pending.append(copy)

    loads[0].wait()
    rows = SEG_DEV * HEADS_DEV
    blocks = LENGTH // BLOCK
    decay = jnp.concatenate([ldec[q] for q in range(SEG_DEV)], axis=0)
    stacked = jnp.concatenate([decay[:, b * BLOCK : (b + 1) * BLOCK] for b in range(blocks)], axis=0)
    top, rest = stacked.astype(BF16), None
    rest = stacked - top.astype(F32)
    middle, low = split(rest)
    earlier = lax.broadcasted_iota(jnp.int32, (BLOCK, BLOCK), 0)
    later = lax.broadcasted_iota(jnp.int32, (BLOCK, BLOCK), 1)
    causal = earlier <= later
    ones = jnp.where(causal, 1.0, 0.0).astype(BF16)
    sums = dot(low, ones) + dot(middle, ones) + dot(top, ones)
    base = jnp.zeros((rows, 1), F32)
    pieces = []
    for b in range(blocks):
        piece = sums[b * rows : (b + 1) * rows] + base
        pieces.append(piece)
        base = piece[:, BLOCK - 1 : BLOCK]
    cumulative = jnp.concatenate(pieces, axis=1)
    cum_row[...] = cumulative
    columns = jnp.concatenate(
        [jnp.exp(base - cumulative), jnp.exp(cumulative), cumulative, jnp.zeros_like(cumulative)], axis=0
    )
    columns = jnp.transpose(columns)
    cum_col[...] = columns
    upper, lower = split(columns)
    for load in loads[1:4]:
        load.wait()
    key_row = lax.broadcasted_iota(jnp.int32, (4 * rows, 2 * WIDTH), 0)
    key_lane = lax.broadcasted_iota(jnp.int32, (4 * rows, 2 * WIDTH), 1)
    lane64 = lax.rem(lax.broadcasted_iota(jnp.int32, (1, WIDTH), 1), HEAD_DIM)
    packed = None
    starts = []
    for q in range(SEG_DEV):
        wanted = (key_lane // WIDTH) * rows + q * HEADS_DEV + lax.rem(key_lane, WIDTH) // HEAD_DIM
        pick = jnp.where(key_row == wanted, 1.0, 0.0).astype(BF16)
        spread = dot(upper, pick) + dot(lower, pick)
        to_end, from_start = spread[:, :WIDTH], spread[:, WIDTH:]
        weight_end[q] = to_end
        starts.append(from_start)
        s_in = (inputs[q].astype(F32) * to_end).astype(BF16)
        scaled_in[q] = s_in
        local_end = dot_tn(sin[q], s_in)
        segment = slots[s * SEG_DEV + q]
        end_decay = jnp.where(lane64 == segment, from_start[LENGTH - 1 : LENGTH], 0.0)
        packed = end_decay if q == 0 else packed + end_decay
        for half in range(2):
            lanes = slice(half * BLOCK, (half + 1) * BLOCK)
            place = pl.ds(q * SLICE, SLICE)
            send1f[half, :, place, :] = local_end[:, lanes].reshape(RING, SLICE, BLOCK)
    for half in range(2):
        row = packed[:, half * BLOCK : (half + 1) * BLOCK].reshape(1, 1, BLOCK)
        send1f[half, :, pl.ds(ROW1, 1), :] = jnp.broadcast_to(row, (RING, 1, BLOCK))

    pl.semaphore_wait(barrier, len(peers))

    rows1 = (pl.ds(0, ROW1 + 1), pl.ds(0, ROW1))
    out1, in1 = (send1f, send1j), (recv1f, recv1j)

    def first(chunk):
        for i in ORDER[:-1]:
            for half in range(2):
                to = lax.rem(mine[half] + i, RING)
                send(
                    out1[chunk].at[half, to, rows1[chunk]], in1[chunk].at[half, i, rows1[chunk]],
                    chunk, (first_peer(half, i), x),
                )
        for half in range(2):
            in1[chunk][half, 0, rows1[chunk]] = out1[chunk][half, mine[half], rows1[chunk]]

    first(0)

    for load in loads[4:]:
        load.wait()
    for q in range(SEG_DEV):
        s_cot = (cotan[q].astype(F32) * starts[q]).astype(BF16)
        scaled_cot[q] = s_cot
        local_adj = dot_tn(sout[q], s_cot)
        for half in range(2):
            lanes = slice(half * BLOCK, (half + 1) * BLOCK)
            place = pl.ds(q * SLICE, SLICE)
            send1j[half, :, place, :] = local_adj[:, lanes].reshape(RING, SLICE, BLOCK)

    lane = lax.broadcasted_iota(jnp.int32, (BLOCK, BLOCK), 1)
    first_head = lane < HEAD_DIM
    for q in range(SEG_DEV):
        for b in range(blocks):
            u0 = b * BLOCK
            length = LENGTH - u0
            here = pl.ds(u0, BLOCK)
            onward = pl.ds(u0, length)
            sin_b = sin[q, here]
            sout_b = sout[q, onward]
            scores = dot_nt(sin_b, sout_b)
            coupled = None
            for pair in range(HEADS_DEV // 2):
                lanes = pl.ds(pair * BLOCK, BLOCK)
                in_pair = inputs[q, here, lanes]
                cot_pair = cotan[q, onward, lanes]
                results = []
                for k in range(2):
                    r = q * HEADS_DEV + pair * 2 + k
                    col = 2 * rows + r
                    spread = cum_row[r : r + 1, onward] - cum_col[here, col : col + 1]
                    mask = jnp.where(causal, jnp.exp(jnp.where(causal, spread[:, :BLOCK], 0.0)), 0.0)
                    if length > BLOCK:
                        mask = jnp.concatenate([mask, jnp.exp(spread[:, BLOCK:])], axis=1)
                    weights = (mask * scores).astype(BF16)
                    results.append(dot(weights, cot_pair))
                    own = first_head if k == 0 else jnp.logical_not(first_head)
                    in_head = jnp.where(own, in_pair.astype(F32), 0.0).astype(BF16)
                    term = mask * dot_nt(in_head, cot_pair)
                    coupled = term if coupled is None else coupled + term
                quad_in[q, here, lanes] = jnp.where(first_head, results[0], results[1])
            if q == 0 and b == ADJ_AFTER:
                first(1)
            coupled = coupled.astype(BF16)
            part[0, q, here] = dot(coupled, sout_b)
            read = dot_tn(coupled, sin_b)
            if b == 0:
                part[1, q] = read
            else:
                part[1, q, onward] = part[1, q, onward] + read

    rank = lax.broadcasted_iota(jnp.int32, (TABLE, SLICE, BLOCK), 0)
    rank_row = lax.broadcasted_iota(jnp.int32, (TABLE, BLOCK), 0)
    rank_lane = lax.rem(lane[:TABLE], HEAD_DIM)
    left = lane[:TABLE] < HEAD_DIM
    rows2 = (pl.ds(0, TABLE + 1), pl.ds(0, TABLE))
    out2, in2 = (send2f, send2j), (recv2f, recv2j)
    decays = [None, None]

    def second(chunk):
        arrive(chunk, in1[chunk].at[:, pl.ds(1, RING - 1), rows1[chunk]])
        out, into = out2[chunk], in2[chunk]
        for half in range(2):
            total = jnp.zeros((TABLE, SLICE, BLOCK), F32)
            for i in range(RING):
                for q in range(SEG_DEV):
                    index = slots[source_seg(half, i) * SEG_DEV + q]
                    if chunk == 1:
                        index = parents[index]
                    block = in1[chunk][half, i, pl.ds(q * SLICE, SLICE)]
                    total = total + jnp.where(rank == index, block[None], 0.0)
            for k in range(TABLE):
                out[half, :, k, :] = total[k]
            if chunk == 0:
                row = recv1f[half, 0, pl.ds(ROW1, 1)]
                for i in range(1, RING):
                    row = row + recv1f[half, i, pl.ds(ROW1, 1)]
                out[half, :, pl.ds(TABLE, 1), :] = jnp.broadcast_to(
                    row.reshape(1, 1, BLOCK), (SLICE, 1, BLOCK)
                )
            for i in ORDER:
                for k in range(CORES):
                    to = lax.rem(other[half] + i, RING) * CORES + lax.rem(c + k, CORES)
                    slot = i * CORES + k
                    if slot == 0:
                        into[half, 0, rows2[chunk]] = out[half, to, rows2[chunk]]
                        continue
                    send(
                        out.at[half, to, rows2[chunk]], into.at[half, slot, rows2[chunk]],
                        2 + chunk, (second_peer(half, i, k), x),
                    )

    def third(chunk):
        into = in2[chunk]
        arrive(2 + chunk, into.at[:, pl.ds(1, SLICE - 1), rows2[chunk]])
        for half in range(2):
            total = into[half, 0, pl.ds(0, TABLE)]
            for slot in range(1, SLICE):
                total = total + into[half, slot, pl.ds(0, TABLE)]
            if chunk == 0:
                row = into[half, 0, pl.ds(TABLE, 1)]
                for slot in range(1, SLICE):
                    row = row + into[half, slot, pl.ds(TABLE, 1)]
                spread = jnp.where(rank_lane == rank_row, row, 0.0)
                first = jnp.sum(jnp.where(left, spread, 0.0), axis=1, keepdims=True)
                second_head = jnp.sum(jnp.where(left, 0.0, spread), axis=1, keepdims=True)
                decays[half] = jnp.where(left, first, second_head)
                carried = jnp.zeros((TABLE, BLOCK), F32)
                for m in range(ROOTS, TABLE):
                    start = jnp.where(parents[m] == 0, total[0:1], total[1:2])
                    carried = carried + jnp.where(rank_row == m, start, 0.0)
                send3[chunk, half] = total + decays[half] * carried
            else:
                carried = jnp.zeros((TABLE, BLOCK), F32)
                product = decays[half] * total
                for m in range(ROOTS, TABLE):
                    carried = carried + jnp.where(rank_row == parents[m], product[m : m + 1], 0.0)
                send3[chunk, half] = total + jnp.where(rank_row < ROOTS, carried, 0.0)
            row = other[half] * CORES + c
            for i in ORDER:
                for k in range(CORES):
                    if i + k == 0:
                        recv3[chunk, half, row] = send3[chunk, half]
                        continue
                    send(
                        send3.at[chunk, half], recv3.at[chunk, half, row],
                        4 + chunk, (second_peer(half, i, k), x),
                    )

    def fourth(chunk):
        arrive(4 + chunk, recv3.at[chunk, :, pl.ds(0, SLICE - 1)])
        for half in range(2):
            for k in range(TABLE):
                table[chunk, half, k] = recv3[chunk, half, :, k, :]
        for q in range(SEG_DEV):
            for i in ORDER:
                for half in range(2):
                    segment = slots[first_peer(half, i) * SEG_DEV + q]
                    if chunk == 0:
                        index = parents[segment]
                        exists = index >= 0
                        index = jnp.maximum(index, 0)
                    else:
                        exists = segment < TABLE
                        index = jnp.minimum(segment, TABLE - 1)
                    picked = jnp.where(exists, table[chunk, half, index], 0.0)
                    row = mine[half]
                    if i == 0:
                        recv4[chunk, q, half, row] = picked
                        continue
                    send4[chunk, q, half, i] = picked
                    send(
                        send4.at[chunk, q, half, i], recv4.at[chunk, q, half, row],
                        6 + 2 * chunk + q, (first_peer(half, i), x),
                    )

    def states_of(chunk):
        kind = 1 - chunk
        states = []
        for q in range(SEG_DEV):
            arrive(6 + 2 * chunk + q, recv4.at[chunk, q, :, pl.ds(0, RING - 1)])
            halves = [recv4[chunk, q, half].reshape(STATE, BLOCK) for half in range(2)]
            state = jnp.concatenate(halves, axis=1).astype(BF16)
            states.append(state)
            data = scaled_cot[q] if chunk == 0 else scaled_in[q]
            part[kind, q] = part[kind, q] + dot_nt(data, state)
            for i in (2, 1, 3):
                to = lax.rem(x + i, HEAD_DEVS)
                piece = pl.ds(pl.multiple_of(to * BLOCK, BLOCK), BLOCK)
                send(part.at[kind, q, piece], recvx.at[kind, q, i], 10 + 2 * chunk + q, (s, to))
        return states

    own = pl.ds(pl.multiple_of(x * BLOCK, BLOCK), BLOCK)

    def heads_of(chunk):
        kind = 1 - chunk
        near, far = ((out_sin, grad_sin), (out_sout, grad_sout))[kind]
        for q in range(SEG_DEV):
            arrive(10 + 2 * chunk + q, recvx.at[kind, q, pl.ds(1, HEAD_DEVS - 1)])
            total = part[kind, q, own]
            for i in range(1, HEAD_DEVS):
                total = total + recvx[kind, q, i]
            near[q] = total
            store = pltpu.make_async_copy(near.at[q], far.at[q], osem.at[2 * kind + q])
            store.start()
            stores.append(store)

    second(0)
    second(1)
    third(0)
    third(1)
    fourth(0)
    fourth(1)
    states_of(0)
    adjoints = states_of(1)
    for q in range(SEG_DEV):
        term = weight_end[q] * dot(sin[q], adjoints[q])
        out_in[q] = (quad_in[q] + term).astype(BF16)
    stores = [pltpu.make_async_copy(out_in, grad_in, osem.at[4])]
    stores[0].start()
    for chunk in range(2):
        heads_of(chunk)
    for store in stores:
        store.wait()
    for copy in pending:
        copy.wait_send()


def hand_over(a_in, b_in, c_in, a_out, b_out, c_out, a, b, c, isem, osem):
    pairs = ((a_in, a), (b_in, b), (c_in, c))
    loads = [pltpu.make_async_copy(far, near, isem.at[n]) for n, (far, near) in enumerate(pairs)]
    pairs = ((a, a_out), (b, b_out), (c, c_out))
    stores = [pltpu.make_async_copy(near, far, osem.at[n]) for n, (near, far) in enumerate(pairs)]
    for load in loads:
        load.start()
    for load, store in zip(loads, stores):
        load.wait()
        store.start()
    for store in stores:
        store.wait()


def shards(inputs, cotangent, state_in, state_out, log_decay, parents, slot_segment):
    hbm = pl.BlockSpec(memory_space=pltpu.HBM)
    both = SEG_DEV * HEADS_DEV
    slots2 = RING * CORES
    dma = pltpu.SemaphoreType.DMA
    grad_state = (SEG_DEV, BLOCK, STATE)
    shapes = (
        jax.ShapeDtypeStruct(inputs.shape, BF16),
        jax.ShapeDtypeStruct(grad_state, F32),
        jax.ShapeDtypeStruct(grad_state, F32),
    )
    results = pl.pallas_call(
        kernel,
        out_shape=shapes,
        in_specs=[hbm] * 7,
        out_specs=(hbm,) * 3,
        scratch_shapes=[
            pltpu.VMEM(inputs.shape, BF16),
            pltpu.VMEM(inputs.shape, BF16),
            pltpu.VMEM(state_in.shape, BF16),
            pltpu.VMEM(state_in.shape, BF16),
            pltpu.VMEM(log_decay.shape, F32),
            pltpu.SMEM(parents.shape, jnp.int32),
            pltpu.SMEM(parents.shape, jnp.int32),
            dma((7,)),
            pltpu.VMEM((both, LENGTH), F32),
            pltpu.VMEM((LENGTH, 4 * both), F32),
            pltpu.VMEM((SEG_DEV, LENGTH, WIDTH), F32),
            pltpu.VMEM((SEG_DEV, LENGTH, WIDTH), BF16),
            pltpu.VMEM((SEG_DEV, LENGTH, WIDTH), BF16),
            pltpu.VMEM((SEG_DEV, LENGTH, WIDTH), F32),
            pltpu.VMEM((2, SEG_DEV, LENGTH, STATE), F32),
            pltpu.VMEM((2, RING, ROW1 + 8, BLOCK), F32),
            pltpu.VMEM((2, RING, ROW1 + 8, BLOCK), F32),
            pltpu.VMEM((2, RING, ROW1, BLOCK), F32),
            pltpu.VMEM((2, RING, ROW1, BLOCK), F32),
            pltpu.VMEM((2, SLICE, 2 * TABLE, BLOCK), F32),
            pltpu.VMEM((2, slots2, 2 * TABLE, BLOCK), F32),
            pltpu.VMEM((2, SLICE, TABLE, BLOCK), F32),
            pltpu.VMEM((2, slots2, TABLE, BLOCK), F32),
            pltpu.VMEM((2, 2, TABLE, BLOCK), F32),
            pltpu.VMEM((2, 2, SLICE, TABLE, BLOCK), F32),
            pltpu.VMEM((2, 2, TABLE, SLICE, BLOCK), F32),
            pltpu.VMEM((2, SEG_DEV, 2, RING, SLICE, BLOCK), F32),
            pltpu.VMEM((2, SEG_DEV, 2, RING, SLICE, BLOCK), F32),
            pltpu.VMEM((2, SEG_DEV, HEAD_DEVS, BLOCK, STATE), F32),
            pltpu.VMEM(inputs.shape, BF16),
            pltpu.VMEM(grad_state, F32),
            pltpu.VMEM(grad_state, F32),
            dma((14,)), dma((14,)), dma((5,)),
        ],
        compiler_params=pltpu.CompilerParams(
            collective_id=0, has_side_effects=True, vmem_limit_bytes=60 * 2**20
        ),
    )(inputs, cotangent, state_in, state_out, log_decay, parents, slot_segment)
    return pl.pallas_call(
        hand_over,
        out_shape=shapes,
        in_specs=[hbm] * 3,
        out_specs=(hbm,) * 3,
        scratch_shapes=[pltpu.VMEM(r.shape, r.dtype) for r in results] + [dma((3,)), dma((3,))],
        compiler_params=pltpu.CompilerParams(vmem_limit_bytes=60 * 2**20),
    )(*results)


def solution(mesh):
    placed = (
        P("seg", None, "head"),
        P("seg", None, "head"),
        P("seg", None, None),
        P("seg", None, None),
        P("seg", "head", None),
        P(),
        P(),
    )
    return jax.shard_map(
        shards,
        mesh=mesh,
        in_specs=placed,
        out_specs=(P("seg", None, "head"), P("seg", "head", None), P("seg", "head", None)),
        check_vma=False,
    )
```

```python
import jax
import jax.numpy as jnp
from jax import lax
from jax.experimental import pallas as pl
from jax.experimental.pallas import tpu as pltpu
from jax.sharding import PartitionSpec as P

MESH = pl.DeviceIdType.MESH
F32 = jnp.float32
BF16 = jnp.bfloat16

ROOTS = 2
TABLE = 8
RING = 8
ORDER = (4, 3, 5, 2, 6, 1, 7, 0)
CORES = 2
HEAD_DEVS = 4
SEG_DEV = 2
LENGTH = 512
HEADS_DEV = 4
HEAD_DIM = 64
WIDTH = HEADS_DEV * HEAD_DIM
STATE = 128
SLICE = STATE // RING
BLOCK = 128
ADJ_AFTER = 1
ROW1 = SEG_DEV * SLICE


def dot(a, b):
    return jnp.dot(a, b, preferred_element_type=F32)


def dot_nt(a, b):
    return lax.dot_general(a, b, (((1,), (1,)), ((), ())), preferred_element_type=F32)


def dot_tn(a, b):
    return lax.dot_general(a, b, (((0,), (0,)), ((), ())), preferred_element_type=F32)


def seg_index(y, z, c):
    return (y * RING + z) * CORES + c


def split(value):
    upper = value.astype(BF16)
    return upper, (value - upper.astype(F32)).astype(BF16)


def kernel(
    inputs_hbm, cotan_hbm, sin_hbm, sout_hbm, ldec_hbm, parents_hbm, slots_hbm,
    grad_in, grad_sin, grad_sout,
    inputs, cotan, sin, sout, ldec, parents, slots, lsem,
    cum_row, cum_col, weight_end, scaled_in, scaled_cot, quad_in, part,
    send1f, recv1f, send1j, recv1j, send2f, recv2f, send2j, recv2j,
    send3, recv3, table, send4, recv4, recvx,
    out_in, out_sin, out_sout, sent, arrived, osem,
):
    s = lax.axis_index("seg")
    x = lax.axis_index("head")
    c = lax.rem(s, CORES)
    z = lax.rem(s // CORES, RING)
    y = s // (CORES * RING)

    mine = (y, z)
    other = (z, y)

    def first_peer(half, i):
        if half == 0:
            return seg_index(lax.rem(y + i, RING), z, c)
        return seg_index(y, lax.rem(z + i, RING), c)

    def second_peer(half, i, k):
        ck = lax.rem(c + k, CORES)
        if half == 0:
            return seg_index(y, lax.rem(z + i, RING), ck)
        return seg_index(lax.rem(y + i, RING), z, ck)

    def source_seg(half, i):
        if half == 0:
            return seg_index(lax.rem(y + RING - i, RING), z, c)
        return seg_index(y, lax.rem(z + RING - i, RING), c)

    loads = []
    operands = (
        (ldec_hbm, ldec), (inputs_hbm, inputs), (sin_hbm, sin), (slots_hbm, slots),
        (cotan_hbm, cotan), (sout_hbm, sout), (parents_hbm, parents),
    )
    for n, (far, near) in enumerate(operands):
        load = pltpu.make_async_copy(far, near, lsem.at[n])
        loads.append(load)
    for load in loads[:4]:
        load.start()

    barrier = pltpu.get_barrier_semaphore()
    peers = []
    for i in ORDER[:-1]:
        for half in range(2):
            for k in range(CORES):
                peers.append((second_peer(half, i, k), x))
    peers.append((seg_index(y, z, lax.rem(c + 1, CORES)), x))
    for i in range(1, HEAD_DEVS):
        peers.append((s, lax.rem(x + i, HEAD_DEVS)))
    for peer in peers:
        pl.semaphore_signal(barrier, inc=1, device_id=peer, device_id_type=MESH)
    for load in loads[4:]:
        load.start()

    pending = []

    def send(src, dst, stage, peer):
        pltpu.make_async_remote_copy(
            src_ref=src, dst_ref=dst, send_sem=sent.at[stage], recv_sem=arrived.at[stage],
            device_id=peer, device_id_type=MESH,
        ).start()

    def arrive(stage, whole):
        copy = pltpu.make_async_remote_copy(
            src_ref=whole, dst_ref=whole, send_sem=sent.at[stage], recv_sem=arrived.at[stage],
            device_id=(seg_index(y, z, lax.rem(c + 1, CORES)), x), device_id_type=MESH,
        )
        copy.wait_recv()
        pending.append(copy)

    loads[0].wait()
    rows = SEG_DEV * HEADS_DEV
    blocks = LENGTH // BLOCK
    decay = jnp.concatenate([ldec[q] for q in range(SEG_DEV)], axis=0)
    stacked = jnp.concatenate([decay[:, b * BLOCK : (b + 1) * BLOCK] for b in range(blocks)], axis=0)
    top, rest = stacked.astype(BF16), None
    rest = stacked - top.astype(F32)
    middle, low = split(rest)
    earlier = lax.broadcasted_iota(jnp.int32, (BLOCK, BLOCK), 0)
    later = lax.broadcasted_iota(jnp.int32, (BLOCK, BLOCK), 1)
    causal = earlier <= later
    ones = jnp.where(causal, 1.0, 0.0).astype(BF16)
    sums = dot(low, ones) + dot(middle, ones) + dot(top, ones)
    base = jnp.zeros((rows, 1), F32)
    pieces = []
    for b in range(blocks):
        piece = sums[b * rows : (b + 1) * rows] + base
        pieces.append(piece)
        base = piece[:, BLOCK - 1 : BLOCK]
    cumulative = jnp.concatenate(pieces, axis=1)
    cum_row[...] = cumulative
    columns = jnp.concatenate(
        [jnp.exp(base - cumulative), jnp.exp(cumulative), cumulative, jnp.zeros_like(cumulative)], axis=0
    )
    columns = jnp.transpose(columns)
    cum_col[...] = columns
    upper, lower = split(columns)
    for load in loads[1:4]:
        load.wait()
    key_row = lax.broadcasted_iota(jnp.int32, (4 * rows, 2 * WIDTH), 0)
    key_lane = lax.broadcasted_iota(jnp.int32, (4 * rows, 2 * WIDTH), 1)
    lane64 = lax.rem(lax.broadcasted_iota(jnp.int32, (1, WIDTH), 1), HEAD_DIM)
    packed = None
    starts = []
    for q in range(SEG_DEV):
        wanted = (key_lane // WIDTH) * rows + q * HEADS_DEV + lax.rem(key_lane, WIDTH) // HEAD_DIM
        pick = jnp.where(key_row == wanted, 1.0, 0.0).astype(BF16)
        spread = dot(upper, pick) + dot(lower, pick)
        to_end, from_start = spread[:, :WIDTH], spread[:, WIDTH:]
        weight_end[q] = to_end
        starts.append(from_start)
        s_in = (inputs[q].astype(F32) * to_end).astype(BF16)
        scaled_in[q] = s_in
        local_end = dot_tn(sin[q], s_in)
        segment = slots[s * SEG_DEV + q]
        end_decay = jnp.where(lane64 == segment, from_start[LENGTH - 1 : LENGTH], 0.0)
        packed = end_decay if q == 0 else packed + end_decay
        for half in range(2):
            lanes = slice(half * BLOCK, (half + 1) * BLOCK)
            place = pl.ds(q * SLICE, SLICE)
            send1f[half, :, place, :] = local_end[:, lanes].reshape(RING, SLICE, BLOCK)
    for half in range(2):
        row = packed[:, half * BLOCK : (half + 1) * BLOCK].reshape(1, 1, BLOCK)
        send1f[half, :, pl.ds(ROW1, 1), :] = jnp.broadcast_to(row, (RING, 1, BLOCK))

    pl.semaphore_wait(barrier, len(peers))

    rows1 = (pl.ds(0, ROW1 + 1), pl.ds(0, ROW1))
    out1, in1 = (send1f, send1j), (recv1f, recv1j)

    def first(chunk):
        for i in ORDER[:-1]:
            for half in range(2):
                to = lax.rem(mine[half] + i, RING)
                send(
                    out1[chunk].at[half, to, rows1[chunk]], in1[chunk].at[half, i, rows1[chunk]],
                    chunk, (first_peer(half, i), x),
                )
        for half in range(2):
            in1[chunk][half, 0, rows1[chunk]] = out1[chunk][half, mine[half], rows1[chunk]]

    first(0)

    for load in loads[4:]:
        load.wait()
    for q in range(SEG_DEV):
        s_cot = (cotan[q].astype(F32) * starts[q]).astype(BF16)
        scaled_cot[q] = s_cot
        local_adj = dot_tn(sout[q], s_cot)
        for half in range(2):
            lanes = slice(half * BLOCK, (half + 1) * BLOCK)
            place = pl.ds(q * SLICE, SLICE)
            send1j[half, :, place, :] = local_adj[:, lanes].reshape(RING, SLICE, BLOCK)

    lane = lax.broadcasted_iota(jnp.int32, (BLOCK, BLOCK), 1)
    first_head = lane < HEAD_DIM
    for q in range(SEG_DEV):
        for b in range(blocks):
            u0 = b * BLOCK
            length = LENGTH - u0
            here = pl.ds(u0, BLOCK)
            onward = pl.ds(u0, length)
            sin_b = sin[q, here]
            sout_b = sout[q, onward]
            scores = dot_nt(sin_b, sout_b)
            coupled = None
            for pair in range(HEADS_DEV // 2):
                lanes = pl.ds(pair * BLOCK, BLOCK)
                in_pair = inputs[q, here, lanes]
                cot_pair = cotan[q, onward, lanes]
                results = []
                for k in range(2):
                    r = q * HEADS_DEV + pair * 2 + k
                    col = 2 * rows + r
                    spread = cum_row[r : r + 1, onward] - cum_col[here, col : col + 1]
                    mask = jnp.where(causal, jnp.exp(jnp.where(causal, spread[:, :BLOCK], 0.0)), 0.0)
                    if length > BLOCK:
                        mask = jnp.concatenate([mask, jnp.exp(spread[:, BLOCK:])], axis=1)
                    weights = (mask * scores).astype(BF16)
                    results.append(dot(weights, cot_pair))
                    own = first_head if k == 0 else jnp.logical_not(first_head)
                    in_head = jnp.where(own, in_pair.astype(F32), 0.0).astype(BF16)
                    term = mask * dot_nt(in_head, cot_pair)
                    coupled = term if coupled is None else coupled + term
                quad_in[q, here, lanes] = jnp.where(first_head, results[0], results[1])
            if q == 0 and b == ADJ_AFTER:
                first(1)
            coupled = coupled.astype(BF16)
            part[0, q, here] = dot(coupled, sout_b)
            read = dot_tn(coupled, sin_b)
            if b == 0:
                part[1, q] = read
            else:
                part[1, q, onward] = part[1, q, onward] + read

    rank = lax.broadcasted_iota(jnp.int32, (TABLE, SLICE, BLOCK), 0)
    rank_row = lax.broadcasted_iota(jnp.int32, (TABLE, BLOCK), 0)
    rank_lane = lax.rem(lane[:TABLE], HEAD_DIM)
    left = lane[:TABLE] < HEAD_DIM
    rows2 = (pl.ds(0, TABLE + 1), pl.ds(0, TABLE))
    out2, in2 = (send2f, send2j), (recv2f, recv2j)
    decays = [None, None]

    def second(chunk):
        arrive(chunk, in1[chunk].at[:, pl.ds(1, RING - 1), rows1[chunk]])
        out, into = out2[chunk], in2[chunk]
        for half in range(2):
            total = jnp.zeros((TABLE, SLICE, BLOCK), F32)
            for i in range(RING):
                for q in range(SEG_DEV):
                    index = slots[source_seg(half, i) * SEG_DEV + q]
                    if chunk == 1:
                        index = parents[index]
                    block = in1[chunk][half, i, pl.ds(q * SLICE, SLICE)]
                    total = total + jnp.where(rank == index, block[None], 0.0)
            for k in range(TABLE):
                out[half, :, k, :] = total[k]
            if chunk == 0:
                row = recv1f[half, 0, pl.ds(ROW1, 1)]
                for i in range(1, RING):
                    row = row + recv1f[half, i, pl.ds(ROW1, 1)]
                out[half, :, pl.ds(TABLE, 1), :] = jnp.broadcast_to(
                    row.reshape(1, 1, BLOCK), (SLICE, 1, BLOCK)
                )
            for i in ORDER:
                for k in range(CORES):
                    to = lax.rem(other[half] + i, RING) * CORES + lax.rem(c + k, CORES)
                    slot = i * CORES + k
                    if slot == 0:
                        into[half, 0, rows2[chunk]] = out[half, to, rows2[chunk]]
                        continue
                    send(
                        out.at[half, to, rows2[chunk]], into.at[half, slot, rows2[chunk]],
                        2 + chunk, (second_peer(half, i, k), x),
                    )

    def third(chunk):
        into = in2[chunk]
        arrive(2 + chunk, into.at[:, pl.ds(1, SLICE - 1), rows2[chunk]])
        for half in range(2):
            total = into[half, 0, pl.ds(0, TABLE)]
            for slot in range(1, SLICE):
                total = total + into[half, slot, pl.ds(0, TABLE)]
            if chunk == 0:
                row = into[half, 0, pl.ds(TABLE, 1)]
                for slot in range(1, SLICE):
                    row = row + into[half, slot, pl.ds(TABLE, 1)]
                spread = jnp.where(rank_lane == rank_row, row, 0.0)
                first = jnp.sum(jnp.where(left, spread, 0.0), axis=1, keepdims=True)
                second_head = jnp.sum(jnp.where(left, 0.0, spread), axis=1, keepdims=True)
                decays[half] = jnp.where(left, first, second_head)
                carried = jnp.zeros((TABLE, BLOCK), F32)
                for m in range(ROOTS, TABLE):
                    start = jnp.where(parents[m] == 0, total[0:1], total[1:2])
                    carried = carried + jnp.where(rank_row == m, start, 0.0)
                send3[chunk, half] = total + decays[half] * carried
            else:
                carried = jnp.zeros((TABLE, BLOCK), F32)
                product = decays[half] * total
                for m in range(ROOTS, TABLE):
                    carried = carried + jnp.where(rank_row == parents[m], product[m : m + 1], 0.0)
                send3[chunk, half] = total + jnp.where(rank_row < ROOTS, carried, 0.0)
            row = other[half] * CORES + c
            for i in ORDER:
                for k in range(CORES):
                    if i + k == 0:
                        recv3[chunk, half, row] = send3[chunk, half]
                        continue
                    send(
                        send3.at[chunk, half], recv3.at[chunk, half, row],
                        4 + chunk, (second_peer(half, i, k), x),
                    )

    def fourth(chunk):
        arrive(4 + chunk, recv3.at[chunk, :, pl.ds(0, SLICE - 1)])
        for half in range(2):
            for k in range(TABLE):
                table[chunk, half, k] = recv3[chunk, half, :, k, :]
        for q in range(SEG_DEV):
            for i in ORDER:
                for half in range(2):
                    segment = slots[first_peer(half, i) * SEG_DEV + q]
                    if chunk == 0:
                        index = parents[segment]
                        exists = index >= 0
                        index = jnp.maximum(index, 0)
                    else:
                        exists = segment < TABLE
                        index = jnp.minimum(segment, TABLE - 1)
                    picked = jnp.where(exists, table[chunk, half, index], 0.0)
                    row = mine[half]
                    if i == 0:
                        recv4[chunk, q, half, row] = picked
                        continue
                    send4[chunk, q, half, i] = picked
                    send(
                        send4.at[chunk, q, half, i], recv4.at[chunk, q, half, row],
                        6 + 2 * chunk + q, (first_peer(half, i), x),
                    )

    def states_of(chunk):
        kind = 1 - chunk
        states = []
        for q in range(SEG_DEV):
            arrive(6 + 2 * chunk + q, recv4.at[chunk, q, :, pl.ds(0, RING - 1)])
            halves = [recv4[chunk, q, half].reshape(STATE, BLOCK) for half in range(2)]
            state = jnp.concatenate(halves, axis=1).astype(BF16)
            states.append(state)
            data = scaled_cot[q] if chunk == 0 else scaled_in[q]
            part[kind, q] = part[kind, q] + dot_nt(data, state)
            for i in (2, 1, 3):
                to = lax.rem(x + i, HEAD_DEVS)
                piece = pl.ds(pl.multiple_of(to * BLOCK, BLOCK), BLOCK)
                send(part.at[kind, q, piece], recvx.at[kind, q, i], 10 + 2 * chunk + q, (s, to))
        return states

    own = pl.ds(pl.multiple_of(x * BLOCK, BLOCK), BLOCK)

    def heads_of(chunk):
        kind = 1 - chunk
        near, far = ((out_sin, grad_sin), (out_sout, grad_sout))[kind]
        for q in range(SEG_DEV):
            arrive(10 + 2 * chunk + q, recvx.at[kind, q, pl.ds(1, HEAD_DEVS - 1)])
            total = part[kind, q, own]
            for i in range(1, HEAD_DEVS):
                total = total + recvx[kind, q, i]
            near[q] = total
            store = pltpu.make_async_copy(near.at[q], far.at[q], osem.at[2 * kind + q])
            store.start()
            stores.append(store)

    second(0)
    second(1)
    third(0)
    third(1)
    fourth(0)
    fourth(1)
    states_of(0)
    adjoints = states_of(1)
    for q in range(SEG_DEV):
        term = weight_end[q] * dot(sin[q], adjoints[q])
        out_in[q] = (quad_in[q] + term).astype(BF16)
    stores = [pltpu.make_async_copy(out_in, grad_in, osem.at[4])]
    stores[0].start()
    for chunk in range(2):
        heads_of(chunk)
    for store in stores:
        store.wait()
    for copy in pending:
        copy.wait_send()


def hand_over(a_in, b_in, c_in, a_out, b_out, c_out, a, b, c, isem, osem):
    steps = [(a_in.at[q], a.at[q], a_out.at[q]) for q in range(SEG_DEV)]
    steps += [(b_in, b, b_out), (c_in, c, c_out)]
    loads = [pltpu.make_async_copy(u, v, isem.at[n]) for n, (u, v, _) in enumerate(steps)]
    stores = [pltpu.make_async_copy(v, w, osem.at[n]) for n, (_, v, w) in enumerate(steps)]
    for load in loads:
        load.start()
    for load, store in zip(loads, stores):
        load.wait()
        store.start()
    for store in stores:
        store.wait()


def shards(inputs, cotangent, state_in, state_out, log_decay, parents, slot_segment):
    hbm = pl.BlockSpec(memory_space=pltpu.HBM)
    both = SEG_DEV * HEADS_DEV
    slots2 = RING * CORES
    dma = pltpu.SemaphoreType.DMA
    grad_state = (SEG_DEV, BLOCK, STATE)
    shapes = (
        jax.ShapeDtypeStruct(inputs.shape, BF16),
        jax.ShapeDtypeStruct(grad_state, F32),
        jax.ShapeDtypeStruct(grad_state, F32),
    )
    results = pl.pallas_call(
        kernel,
        out_shape=shapes,
        in_specs=[hbm] * 7,
        out_specs=(hbm,) * 3,
        scratch_shapes=[
            pltpu.VMEM(inputs.shape, BF16),
            pltpu.VMEM(inputs.shape, BF16),
            pltpu.VMEM(state_in.shape, BF16),
            pltpu.VMEM(state_in.shape, BF16),
            pltpu.VMEM(log_decay.shape, F32),
            pltpu.SMEM(parents.shape, jnp.int32),
            pltpu.SMEM(parents.shape, jnp.int32),
            dma((7,)),
            pltpu.VMEM((both, LENGTH), F32),
            pltpu.VMEM((LENGTH, 4 * both), F32),
            pltpu.VMEM((SEG_DEV, LENGTH, WIDTH), F32),
            pltpu.VMEM((SEG_DEV, LENGTH, WIDTH), BF16),
            pltpu.VMEM((SEG_DEV, LENGTH, WIDTH), BF16),
            pltpu.VMEM((SEG_DEV, LENGTH, WIDTH), F32),
            pltpu.VMEM((2, SEG_DEV, LENGTH, STATE), F32),
            pltpu.VMEM((2, RING, ROW1 + 8, BLOCK), F32),
            pltpu.VMEM((2, RING, ROW1 + 8, BLOCK), F32),
            pltpu.VMEM((2, RING, ROW1, BLOCK), F32),
            pltpu.VMEM((2, RING, ROW1, BLOCK), F32),
            pltpu.VMEM((2, SLICE, 2 * TABLE, BLOCK), F32),
            pltpu.VMEM((2, slots2, 2 * TABLE, BLOCK), F32),
            pltpu.VMEM((2, SLICE, TABLE, BLOCK), F32),
            pltpu.VMEM((2, slots2, TABLE, BLOCK), F32),
            pltpu.VMEM((2, 2, TABLE, BLOCK), F32),
            pltpu.VMEM((2, 2, SLICE, TABLE, BLOCK), F32),
            pltpu.VMEM((2, 2, TABLE, SLICE, BLOCK), F32),
            pltpu.VMEM((2, SEG_DEV, 2, RING, SLICE, BLOCK), F32),
            pltpu.VMEM((2, SEG_DEV, 2, RING, SLICE, BLOCK), F32),
            pltpu.VMEM((2, SEG_DEV, HEAD_DEVS, BLOCK, STATE), F32),
            pltpu.VMEM(inputs.shape, BF16),
            pltpu.VMEM(grad_state, F32),
            pltpu.VMEM(grad_state, F32),
            dma((14,)), dma((14,)), dma((5,)),
        ],
        compiler_params=pltpu.CompilerParams(
            collective_id=0, has_side_effects=True, vmem_limit_bytes=60 * 2**20
        ),
    )(inputs, cotangent, state_in, state_out, log_decay, parents, slot_segment)
    return pl.pallas_call(
        hand_over,
        out_shape=shapes,
        in_specs=[hbm] * 3,
        out_specs=(hbm,) * 3,
        scratch_shapes=[pltpu.VMEM(r.shape, r.dtype) for r in results] + [dma((4,)), dma((4,))],
        compiler_params=pltpu.CompilerParams(vmem_limit_bytes=60 * 2**20),
    )(*results)


def solution(mesh):
    placed = (
        P("seg", None, "head"),
        P("seg", None, "head"),
        P("seg", None, None),
        P("seg", None, None),
        P("seg", "head", None),
        P(),
        P(),
    )
    return jax.shard_map(
        shards,
        mesh=mesh,
        in_specs=placed,
        out_specs=(P("seg", None, "head"), P("seg", "head", None), P("seg", "head", None)),
        check_vma=False,
    )
```
